32 devices in a mesh: section: 4 (over x, core), ep: 8 (over z, y).
Axes of the slice: x: 2, y: 2, z: 4, core: 2. Of those that a mesh axis runs over, the one named last changes fastest.
Arguments:
- tokens: bfloat16 [4, 1024, 4096], P('section', 'ep'), may hold values from -6 to 6
- routes: int32 [4, 1024, 8], P('section', 'ep'), may hold values from 0 to 127, as said below
- router_weights: float32 [4, 1024, 8], P('section', 'ep'), may hold values from 0.25 to 1
- w_gate: bfloat16 [4, 8, 4096, 384], P('section', 'ep'), may hold values from -0.09375 to 0.09375
- w_up: bfloat16 [4, 8, 4096, 384], P('section', 'ep'), may hold values from -0.09375 to 0.09375
- w_down: bfloat16 [4, 8, 384, 4096], P('section', 'ep'), may hold values from -0.15625 to 0.15625
- w_query: bfloat16 [4, 4096, 1024], P('section', 'ep'), may hold values from -0.09375 to 0.09375
- w_keyval: bfloat16 [4, 4096, 256], P('section', 'ep'), may hold values from -0.09375 to 0.09375
- gain_query: float32 [4, 128], P('section'), may hold values from 0.8 to 2
- gain_key: float32 [4, 128], P('section'), may hold values from 0.8 to 2
- segment_ids: int32 [4, 1024], P('section', 'ep'), may hold values from 0 to 3, never falling along the last dimension, each value on 1 to 512 neighbouring positions
Outputs:
- layer_out: bfloat16 [4, 1024, 4096], P('section', 'ep')
- attended: bfloat16 [4, 1024, 1024], P('section', 'ep')
The draws below stay inside these ranges and needn't reach their ends.
Inputs may be any that keep to these rules, and one draw needn't show every extreme that they name: `routes`: each token names 8 different experts, at most one of them below 2. Among the tokens of one device (aligned blocks of 128 rows in each section) no expert below 2 is named by more than 64 of them, and in each section one expert below 2 is named by exactly 64 tokens of every block. `segment_ids`: along each section's tokens the reaction numbers never fall; each reaction spans 1 to 512 tokens and one spans exactly 512.
All inputs are finite; a program needn't handle non-finite values.
Results may differ from the reference program's by a relative error of at most 0.018.
Values may be sent and summed in bfloat16 or wider, within the bound.
A program may use at most 128 MiB of HBM per device.

```python
import math
import jax
import jax.numpy as jnp
import numpy as np
from jax import lax

D = 4096
HID = 1536
EXPERTS = 128
TOPK = 8
HD = 128
QH = 8
OWNERS = 4
SEG_MOST = 512
TOK_DEV = 128
SECTIONS = 4
TOKENS = 1024
SEGMENTS = 4
EXP_FLY = 2
CAP = 64
HID_PART = 384
N_EP = 8


def draw_routes(key, part):
    per_section = TOKENS // TOK_DEV
    blocks = SECTIONS * per_section
    subkeys = jax.random.split(jax.random.fold_in(key, 11), 7)
    hot_expert = jax.random.randint(subkeys[0], (SECTIONS, 1), 0, EXP_FLY)
    hot_expert = jnp.broadcast_to(hot_expert, (SECTIONS, per_section)).reshape(blocks)
    shuffled = jax.vmap(lambda subkey: jax.random.permutation(subkey, TOK_DEV))(jax.random.split(subkeys[1], blocks))
    forced = shuffled < CAP
    other_expert = (hot_expert[:, None] + 1 + jax.random.randint(subkeys[2], (blocks, TOK_DEV), 0, EXP_FLY - 1)) % EXP_FLY
    wants_route = (jax.random.randint(subkeys[3], (blocks, TOK_DEV), 0, 2) == 1) & jnp.logical_not(forced)
    expert_ids = jnp.arange(EXP_FLY, dtype=jnp.int32)
    onehot = ((other_expert[..., None] == expert_ids) & wants_route[..., None]).astype(jnp.int32)
    rank_before = jnp.sum((jnp.cumsum(onehot, axis=1) - onehot) * onehot, axis=-1)
    kept_route = wants_route & (rank_before < CAP)
    has_route = forced | kept_route
    held_expert = jnp.where(forced, hot_expert[:, None], other_expert)
    outside_span = EXPERTS - EXP_FLY
    stride = outside_span // TOPK
    start_at = jax.random.randint(subkeys[4], (blocks, TOK_DEV, 1), 0, outside_span)
    jitter = jax.random.randint(subkeys[5], (blocks, TOK_DEV, TOPK), 0, stride)
    outside = EXP_FLY + (start_at + jnp.arange(TOPK, dtype=jnp.int32) * stride + jitter) % outside_span
    placed_at = jax.random.randint(subkeys[6], (blocks, TOK_DEV, 1), 0, TOPK)
    selected = (jnp.arange(TOPK, dtype=jnp.int32) == placed_at) & has_route[..., None]
    routes = jnp.where(selected, held_expert[..., None], outside)
    return routes.reshape(SECTIONS, TOKENS, TOPK).astype(jnp.int32)


def shard_levels(key, dims, cuts, least, top_value):
    level = 1.0
    for axis_at, parts in cuts:
        steps = jax.random.uniform(jax.random.fold_in(jax.random.fold_in(key, 6), axis_at), (parts,), jnp.float32, least / len(cuts), top_value / len(cuts))
        level = level * jnp.repeat(jnp.exp(steps), dims[axis_at] // parts).reshape((-1,) + (1,) * (len(dims) - 1 - axis_at))
    return level


def profile(amount, total, limit, slope):
    weights = [(1 << 20) // math.isqrt(grade ** slope) + 1 for grade in range(2, amount + 1)]
    spare, counts = total - limit - (amount - 1), [1] * (amount - 1)
    while spare > 0:
        candidates = [i for i in range(amount - 1) if counts[i] < limit]
        pool, left = sum([weights[i] for i in candidates]), spare
        for i in candidates:
            more = min(limit - counts[i], max(1, left * weights[i] // pool), spare)
            counts[i] = counts[i] + more
            spare = spare - more
    return np.array([limit] + counts)


def ragged(stream_key, number_of, total, limit, skew):
    if number_of == 2:
        one = jax.random.randint(stream_key, (), max(1, total - limit), min(limit, total - 1) + 1)
        return jnp.stack([one, total - one])
    lengths = jnp.asarray(profile(number_of, total, limit, skew), jnp.int32)
    twos = (number_of - 1) // 2
    source_of, taker = lengths[1:1 + 2 * twos:2], lengths[2:2 + 2 * twos:2]
    margin = jnp.minimum(source_of - 1, limit - taker)
    moved = jax.random.randint(jax.random.fold_in(stream_key, 1), (twos,), 0, 1 << 20) % (margin + 1)
    lengths = lengths.at[1:1 + 2 * twos:2].set(source_of - moved).at[2:2 + 2 * twos:2].set(taker + moved)
    return lengths[jax.random.permutation(jax.random.fold_in(stream_key, 2), number_of)]


def gaussian(key, extent, deviation, bound, shards=(), kind=jnp.bfloat16):
    gain = shard_levels(key, extent, shards, -0.22, 0.18) if shards else 1.0
    result = jax.random.normal(key, extent, jnp.float32) * deviation * gain
    return jnp.minimum(jnp.maximum(result, -bound), bound).astype(kind)


def setup_inputs(seed: int = 0) -> dict:
    arg_keys = jax.random.split(jax.random.key(seed), 12)
    tokens = gaussian(arg_keys[0], (SECTIONS, TOKENS, D), 1.0, 6.0, ((0, 4), (1, 8)))
    routes = draw_routes(jax.random.fold_in(arg_keys[11], 71), 0)
    router_weights = jnp.clip(0.25 + 0.75 * jax.random.uniform(arg_keys[2], (SECTIONS, TOKENS, TOPK), jnp.float32) ** shard_levels(arg_keys[2], (SECTIONS, TOKENS, TOPK), ((0, 4), (1, 8)), -0.2, 0.2), 0.25, 1.0)
    w_gate = gaussian(arg_keys[3], (SECTIONS, EXP_FLY * OWNERS, D, HID_PART), D ** -0.5, 0.09375, ((0, 4), (1, 8)))
    w_up = gaussian(arg_keys[4], (SECTIONS, EXP_FLY * OWNERS, D, HID_PART), D ** -0.5, 0.09375, ((0, 4), (1, 8)))
    w_down = gaussian(arg_keys[5], (SECTIONS, EXP_FLY * OWNERS, HID_PART, D), HID ** -0.5, 0.15625, ((0, 4), (1, 8)))
    w_query = gaussian(arg_keys[6], (SECTIONS, D, QH * HD), D ** -0.5, 0.09375, ((0, 4), (1, 8)))
    w_keyval = gaussian(arg_keys[7], (SECTIONS, D, 2 * HD), D ** -0.5, 0.09375, ((0, 4), (1, 8)))
    gain_query = jnp.clip(jnp.exp(math.log(2.0) - 0.9162907 * jax.random.uniform(arg_keys[8], (SECTIONS, HD), jnp.float32) ** shard_levels(arg_keys[8], (SECTIONS, HD), ((0, 4),), -0.2, 0.2)), 0.8, 2.0)
    gain_key = jnp.clip(jnp.exp(math.log(2.0) - 0.9162907 * jax.random.uniform(arg_keys[9], (SECTIONS, HD), jnp.float32) ** shard_levels(arg_keys[9], (SECTIONS, HD), ((0, 4),), -0.2, 0.2)), 0.8, 2.0)
    segment_ids = jax.vmap(lambda own: jnp.searchsorted(jnp.cumsum(ragged(own, SEGMENTS, TOKENS, SEG_MOST, 1)), jnp.arange(TOKENS), side="right"))(jax.random.split(arg_keys[10], SECTIONS)).reshape((SECTIONS, TOKENS)).astype(jnp.int32)
    return {"tokens": tokens, "routes": routes, "router_weights": router_weights, "w_gate": w_gate, "w_up": w_up, "w_down": w_down, "w_query": w_query, "w_keyval": w_keyval, "gain_query": gain_query, "gain_key": gain_key, "segment_ids": segment_ids}


EPSILON = 1e-06
ROPE_BASE = 1000000.0

def rms_rows(values):
    return values * lax.rsqrt(lax.optimization_barrier(jnp.mean(values * values, axis=-1, keepdims=True)) + EPSILON)

def rotary(values, position):
    half_count = values.shape[-1] // 2
    frequency = ROPE_BASE ** (-(jnp.arange(half_count, dtype=jnp.float32) * 2.0) / values.shape[-1])
    angles = position.astype(jnp.float32)[:, None] * frequency[None, :]
    cosine = jnp.concatenate([jnp.cos(angles), jnp.cos(angles)], axis=-1)[:, None, :]
    sine = jnp.concatenate([jnp.sin(angles), jnp.sin(angles)], axis=-1)[:, None, :]
    turned = jnp.concatenate([-values[..., half_count:], values[..., :half_count]], axis=-1)
    return values * cosine + turned * sine

def expert_layer(tokens, routes, router_weights, w_gate, w_up, w_down):
    wide_tokens = tokens.astype(jnp.float32)
    normed = rms_rows(wide_tokens).astype(jnp.bfloat16)
    inside = routes < EXP_FLY
    has_route = jnp.any(inside, axis=-1)
    chosen = lax.optimization_barrier(jnp.sum(jnp.where(inside, routes, 0), axis=-1)).astype(jnp.int32)
    weight_kept = lax.optimization_barrier(jnp.sum(jnp.where(inside, router_weights, 0.0), axis=-1))
    gate_all = w_gate.reshape(EXP_FLY, OWNERS, D, HID_PART).transpose(0, 2, 1, 3).reshape(EXP_FLY, D, HID)
    up_all = w_up.reshape(EXP_FLY, OWNERS, D, HID_PART).transpose(0, 2, 1, 3).reshape(EXP_FLY, D, HID)
    down_all = w_down.reshape(EXP_FLY, HID, D)

    def one_expert(running, expert_index):
        member = has_route & (chosen == expert_index)
        row_ids = jnp.nonzero(member, size=N_EP * CAP, fill_value=0)[0]
        live_rows = jnp.arange(N_EP * CAP) < jnp.sum(member)
        picked = normed[row_ids]
        gate_proj = jnp.dot(picked, gate_all[expert_index], preferred_element_type=jnp.float32)
        up_proj = jnp.dot(picked, up_all[expert_index], preferred_element_type=jnp.float32)
        activated = (jax.nn.silu(gate_proj) * up_proj).astype(jnp.bfloat16)
        expert_rows = jnp.dot(activated, down_all[expert_index], preferred_element_type=jnp.float32)
        return (running.at[row_ids].add(jnp.where(live_rows[:, None], expert_rows, 0.0)), None)
    expert_out, _ = lax.scan(one_expert, jnp.zeros((TOKENS, D), jnp.float32), jnp.arange(EXP_FLY, dtype=jnp.int32))
    return (wide_tokens + weight_kept[:, None] * expert_out).astype(jnp.bfloat16)

def attention(arrived, w_query, w_keyval, gain_query, gain_key, segment_row):
    lifted = rms_rows(arrived.astype(jnp.float32)).astype(jnp.bfloat16)
    query_raw = jnp.dot(lifted, w_query, preferred_element_type=jnp.float32).reshape(TOKENS, QH, HD)
    keyval_raw = jnp.dot(lifted, w_keyval, preferred_element_type=jnp.float32)
    index_all = jnp.arange(TOKENS, dtype=jnp.int32)
    change = jnp.concatenate([jnp.ones((1,), dtype=bool), segment_row[1:] != segment_row[:-1]])
    starts = lax.cummax(jnp.where(change, index_all, 0).astype(jnp.int32), axis=0).astype(jnp.int32)
    position = (index_all - starts).astype(jnp.int32)
    query = rotary(rms_rows(query_raw) * gain_query, position).astype(jnp.bfloat16)
    key_part = rotary(rms_rows(keyval_raw[:, None, :HD]) * gain_key, position)[:, 0].astype(jnp.bfloat16)
    value_part = keyval_raw[:, HD:].astype(jnp.bfloat16)
    key_wide = lax.optimization_barrier(key_part).astype(jnp.float32)
    value_wide = lax.optimization_barrier(value_part).astype(jnp.float32)
    query_kept = lax.optimization_barrier(query)
    block_rows = math.gcd(TOKENS, 512)
    score_scale = 1.0 / math.sqrt(HD)

    def one_block(block_index):
        first_row = (block_index * block_rows).astype(jnp.int32)
        query_block = lax.dynamic_slice_in_dim(query_kept, first_row, block_rows, 0).astype(jnp.float32)
        query_start = lax.dynamic_slice_in_dim(starts, first_row, block_rows, 0)
        scores = jnp.einsum('qhd,kd->qhk', query_block, key_wide) * score_scale
        query_pos = first_row + jnp.arange(block_rows, dtype=jnp.int32)
        allowed = (index_all[None, None, :] <= query_pos[:, None, None]) & (index_all[None, None, :] >= query_start[:, None, None])
        probabilities = jnp.where(allowed, jnp.exp(scores), 0.0)
        total_mass = lax.optimization_barrier(jnp.sum(probabilities, axis=-1))
        rounded = lax.optimization_barrier(probabilities.astype(jnp.bfloat16)).astype(jnp.float32)
        mixed = jnp.einsum('qhk,kd->qhd', rounded, value_wide) / total_mass[..., None]
        return mixed.astype(jnp.bfloat16).reshape(block_rows, QH * HD)
    return lax.map(one_block, jnp.arange(TOKENS // block_rows, dtype=jnp.int32)).reshape(TOKENS, QH * HD)

def reference(tokens, routes, router_weights, w_gate, w_up, w_down, w_query, w_keyval, gain_query, gain_key, segment_ids):
    section_outs = []
    for section_index in range(SECTIONS):
        section_outs.append(expert_layer(tokens[section_index], routes[section_index], router_weights[section_index], w_gate[section_index], w_up[section_index], w_down[section_index]))
    section_attended = []
    for section_index in range(SECTIONS):
        previous = section_outs[(section_index - 1) % SECTIONS]
        section_attended.append(attention(previous, w_query[section_index], w_keyval[section_index], gain_query[section_index], gain_key[section_index], segment_ids[section_index]))
    return (jnp.stack(section_outs), jnp.stack(section_attended))
```

```python
import math

import jax
import jax.numpy as jnp
from jax import lax
from jax.experimental import pallas as pl
from jax.experimental.pallas import tpu as pltpu
from jax.sharding import PartitionSpec as P

OWNERS = 4
SEG_MOST = 512


EPSILON = 1e-06
ROPE_BASE = 1000000.0
FAR_INDEX = 1073741824


def passed_along(block, axis, distance):
    devices = range(lax.axis_size(axis))
    route = [((i - distance) % len(devices), i) for i in devices]
    return lax.ppermute(block, axis, route)


def prefix(shard, axis, combine, identity):
    length, mine = (lax.axis_size(axis), lax.axis_index(axis))
    everything = jax.tree.map(lambda part: lax.all_gather(part, axis), shard)
    start = jax.tree.map(
        lambda part, zero: jnp.broadcast_to(jnp.asarray(zero, part.dtype), part.shape),
        shard,
        identity,
    )

    def step(k, before):
        reached = k < mine
        new = combine(before, jax.tree.map(lambda part: part[k], everything))
        return jax.tree.map(lambda a, b: jnp.where(reached, a, b), new, before)

    return lax.fori_loop(0, length, step, start)


def passed_along_2(value, axis, steps):
    count = lax.axis_size(axis)
    leading, last = (max(0, -steps), min(count, count - steps))
    return lax.ppermute(value, axis, [(source, source + steps) for source in range(leading, last)])


def rms_rows(values):
    return values * lax.rsqrt(jnp.mean(values * values, axis=-1, keepdims=True) + EPSILON)


def rotary(values, position):
    half_count = values.shape[-1] // 2
    frequency = ROPE_BASE ** (-(jnp.arange(half_count, dtype=jnp.float32) * 2.0) / values.shape[-1])
    angles = position.astype(jnp.float32)[:, None] * frequency[None, :]
    cosine = jnp.concatenate([jnp.cos(angles), jnp.cos(angles)], axis=-1)[:, None, :]
    sine = jnp.concatenate([jnp.sin(angles), jnp.sin(angles)], axis=-1)[:, None, :]
    turned = jnp.concatenate([-values[..., half_count:], values[..., :half_count]], axis=-1)
    return values * cosine + turned * sine


def feed_forward(row_block, gate_part, up_part, down_part):
    gate_proj = jnp.dot(row_block, gate_part, preferred_element_type=jnp.float32)
    up_proj = jnp.dot(row_block, up_part, preferred_element_type=jnp.float32)
    activated = (jax.nn.silu(gate_proj) * up_proj).astype(jnp.bfloat16)
    return jnp.dot(activated, down_part, preferred_element_type=jnp.float32)


def keep_later(earlier, later):
    same_id = earlier[0] == later[0]
    newer_id = later[0] > earlier[0]
    start_at = jnp.where(
        same_id, jnp.minimum(earlier[1], later[1]), jnp.where(newer_id, later[1], earlier[1])
    )
    return (jnp.maximum(earlier[0], later[0]), start_at)


def on_device(
    tokens,
    routes,
    router_weights,
    w_gate,
    w_up,
    w_down,
    w_query,
    w_keyval,
    gain_query,
    gain_key,
    segment_ids,
):
    device_count = lax.axis_size("ep")
    expert_count = device_count // OWNERS
    token_count = tokens.shape[1]
    model_width = tokens.shape[2]
    capacity = OWNERS * max(1, token_count // device_count)
    wide_tokens = tokens[0].astype(jnp.float32)
    normed = rms_rows(wide_tokens).astype(jnp.bfloat16)
    inside = routes[0] < expert_count
    has_route = jnp.any(inside, axis=-1)
    chosen = jnp.sum(jnp.where(inside, routes[0], 0), axis=-1)
    weight_kept = jnp.sum(jnp.where(inside, router_weights[0], 0.0), axis=-1)
    expert_ids = jnp.arange(expert_count, dtype=jnp.int32)
    member = ((chosen[:, None] == expert_ids[None, :]) & has_route[:, None]).astype(jnp.int32)
    rank_within = jnp.sum((jnp.cumsum(member, axis=0) - member) * member, axis=-1)
    slot_index = jnp.where(has_route, chosen * capacity + rank_within, -1)
    slot_ids = jnp.arange(expert_count * capacity, dtype=jnp.int32)
    placing = (slot_ids[:, None] == slot_index[None, :]).astype(jnp.bfloat16)
    packed = jnp.dot(placing, normed, preferred_element_type=jnp.float32).astype(jnp.bfloat16)
    gate_part = w_gate[0, 0]
    up_part = w_up[0, 0]
    down_part = w_down[0, 0]
    spread = jnp.broadcast_to(
        packed.reshape(expert_count, 1, capacity, model_width),
        (expert_count, OWNERS, capacity, model_width),
    ).reshape(device_count, capacity, model_width)
    received = lax.all_to_all(spread, "ep", split_axis=0, concat_axis=0, tiled=True)
    partial_out = feed_forward(
        received.reshape(-1, model_width), gate_part, up_part, down_part
    ).reshape(received.shape)
    returned_rows = lax.all_to_all(
        partial_out.astype(jnp.bfloat16), "ep", split_axis=0, concat_axis=0, tiled=True
    ).astype(partial_out.dtype)
    merged = jnp.sum(
        returned_rows.reshape(expert_count, OWNERS, capacity, model_width), axis=1
    ).reshape(expert_count * capacity, model_width)
    fetched_rows = jnp.take(merged, jnp.maximum(slot_index, 0), axis=0)
    expert_out = jnp.where(has_route[:, None], fetched_rows, 0.0)
    layer_out = (wide_tokens + weight_kept[:, None] * expert_out).astype(jnp.bfloat16)
    arrived = passed_along(layer_out, "section", 1)
    lifted = rms_rows(arrived.astype(jnp.float32)).astype(jnp.bfloat16)
    head_dim = gain_query.shape[-1]
    query_width = w_query.shape[-1]
    head_count = query_width // head_dim
    query_raw = jnp.dot(
        lifted,
        lax.all_gather(w_query[0], "ep", axis=0, tiled=True),
        preferred_element_type=jnp.float32,
    )
    keyval_raw = jnp.dot(
        lifted,
        lax.all_gather(w_keyval[0], "ep", axis=0, tiled=True),
        preferred_element_type=jnp.float32,
    )
    segment_row = segment_ids[0]
    first_index = lax.axis_index("ep") * token_count
    global_index = first_index + jnp.arange(token_count, dtype=jnp.int32)
    change = jnp.concatenate([jnp.ones((1,), dtype=bool), segment_row[1:] != segment_row[:-1]])
    local_start = lax.cummax(jnp.where(change, global_index, 0), axis=0)
    empty_prior = (jnp.full((1,), -1, jnp.int32), jnp.full((1,), FAR_INDEX, jnp.int32))
    prior_id, prior_start = prefix(
        (segment_row[-1:], local_start[-1:]), "ep", keep_later, empty_prior
    )
    start_index = jnp.where(segment_row == prior_id[0], prior_start[0], local_start).astype(
        jnp.int32
    )
    position = global_index - start_index
    query = rotary(
        rms_rows(query_raw.reshape(token_count, head_count, head_dim)) * gain_query[0], position
    ).astype(jnp.bfloat16)
    key_part = rotary(rms_rows(keyval_raw[:, None, :head_dim]) * gain_key[0], position)[
        :, 0
    ].astype(jnp.bfloat16)
    value_part = keyval_raw[:, head_dim:].astype(jnp.bfloat16)
    key_value = jnp.concatenate([key_part, value_part], axis=-1)
    reach = (SEG_MOST - 1) // token_count + 1
    earlier_pieces = []
    for distance in range(1, reach + 1):
        earlier_pieces.append(passed_along_2(key_value, "ep", distance))
    window = jnp.concatenate(earlier_pieces[::-1] + [key_value], axis=0)
    key_index = (
        first_index - reach * token_count + jnp.arange((reach + 1) * token_count, dtype=jnp.int32)
    )
    query_rows = query.reshape(token_count * head_count, head_dim)
    query_index = jnp.repeat(global_index, head_count)
    query_start = jnp.repeat(start_index, head_count)
    score_scale = 1.0 / math.sqrt(head_dim)
    scores = (
        jnp.einsum(
            "qd,kd->qk", query_rows, window[:, :head_dim], preferred_element_type=jnp.float32
        )
        * score_scale
    )
    allowed = (key_index[None, :] <= query_index[:, None]) & (
        key_index[None, :] >= query_start[:, None]
    )
    probabilities = jnp.where(allowed, jnp.exp(scores), 0.0)
    total_mass = jnp.sum(probabilities, axis=-1)
    mixed = jnp.dot(
        probabilities.astype(jnp.bfloat16), window[:, head_dim:], preferred_element_type=jnp.float32
    )
    attended = (mixed / total_mass[:, None]).astype(jnp.bfloat16).reshape(token_count, query_width)
    return (layer_out[None], attended[None])


MESH = pl.DeviceIdType.MESH
CHUNKS = 4


def fused_kernel(
    tok_ref, route_ref, rw_ref, wg_hbm, wu_hbm, wd_hbm, wq_hbm, wkv_hbm,
    gq_ref, gk_ref, segrow_ref, segcol_ref, freq_ref,
    lo_ref, att_ref,
    xbuf, other, wgu, wd, act, pd, py, pz, own, r1, r2y, r2z, sm, rm,
    lo, lbuf, wbuf, rbuf, scale_out, scale_in, kv, segs, place_s,
    load_sem, send_sem, recv_sem, l_send, l_recv, p_send, p_recv,
    kv_send, kv_recv, seg_send, seg_recv,
):
    f32, bf16 = jnp.float32, jnp.bfloat16
    section = lax.axis_index("section")
    sections = lax.axis_size("section")
    me = lax.axis_index("ep")
    count = lax.axis_size("ep")
    z, y = me // 2, me % 2
    expert = z // 2
    token_count, width = tok_ref.shape
    half = token_count // 2
    piece = width // CHUNKS
    y_peer = z * 2 + (1 - y)
    z_peer = (z // 2 * 2 + 1 - z % 2) * 2 + y
    mirror = lax.rem(z + 2, 4) * 2 + y
    following = lax.rem(section + 1, sections)
    preceding = lax.rem(section + sections - 1, sections)

    barrier = pltpu.get_barrier_semaphore()
    for k in range(1, 8):
        pl.semaphore_signal(
            barrier, inc=1, device_id=(section, lax.rem(me + k, count)), device_id_type=MESH
        )
    for k in range(4):
        pl.semaphore_signal(barrier, inc=1, device_id=(preceding, k * 2 + y), device_id_type=MESH)

    hidden_parts = wgu.shape[0]
    loads = []
    for j in range(hidden_parts):
        cols = pl.ds(j * 128, 128)
        loads.append((wg_hbm.at[:, cols], wgu.at[j, :, pl.ds(0, 128)]))
        loads.append((wu_hbm.at[:, cols], wgu.at[j, :, pl.ds(128, 128)]))
    loads.append((wd_hbm, wd))
    query_width = wq_hbm.shape[1]
    loads.append((wq_hbm, wbuf.at[y, :, pl.ds(0, query_width)]))
    loads.append((wkv_hbm, wbuf.at[y, :, pl.ds(query_width, wkv_hbm.shape[1])]))
    loads = [
        pltpu.make_async_copy(src, dst, load_sem.at[i]) for i, (src, dst) in enumerate(loads)
    ]
    for load in loads:
        load.start()

    def remote(src, dst, i, target):
        return pltpu.make_async_remote_copy(
            src_ref=src, dst_ref=dst, send_sem=send_sem.at[i], recv_sem=recv_sem.at[i],
            device_id=(section, target), device_id_type=MESH,
        )

    low, high = pl.ds(0, half), pl.ds(half, half)
    c0 = remote(other, xbuf.at[0, high], 0, mirror)
    c1 = remote(xbuf.at[0, low], xbuf.at[1, low], 1, y_peer)
    c2 = remote(xbuf.at[0, low], xbuf.at[2, low], 2, z_peer)
    c3 = remote(xbuf.at[0, high], xbuf.at[1, high], 3, y_peer)
    c4 = remote(xbuf.at[0, high], xbuf.at[2, high], 4, z_peer)
    c5 = remote(xbuf.at[1, low], xbuf.at[3, low], 5, z_peer)
    c6 = remote(xbuf.at[2, high], xbuf.at[3, high], 6, y_peer)
    first_hop = []
    for c in range(CHUNKS):
        first_hop.append(remote(pd.at[c], r1.at[c], 7 + c, z_peer if c < 2 else y_peer))
    to_y = [remote(py.at[c], r2y.at[c], 11 + c, y_peer) for c in range(CHUNKS)]
    to_z = [remote(pz.at[c], r2z.at[c], 15 + c, z_peer) for c in range(CHUNKS)]
    to_mirror = [remote(sm.at[c], rm.at[c], 19 + c, mirror) for c in range(CHUNKS)]
    weights = remote(wbuf.at[y], wbuf.at[y], 23, y_peer)
    weights_in = remote(wbuf.at[1 - y], wbuf.at[1 - y], 23, y_peer)

    squares = jnp.zeros((token_count, 1), f32)
    for c in range(CHUNKS):
        part = tok_ref[:, c * piece : (c + 1) * piece].astype(f32)
        squares += jnp.sum(part * part, axis=-1, keepdims=True)
    inverse = lax.rsqrt(squares / width + EPSILON)
    routes = route_ref[...]
    inside = routes < 2
    has_route = jnp.sum(jnp.where(inside, 1.0, 0.0), axis=-1, keepdims=True)
    chosen = jnp.sum(jnp.where(inside, routes.astype(f32), 0.0), axis=-1, keepdims=True)
    weight = jnp.sum(jnp.where(inside, rw_ref[...], 0.0), axis=-1, keepdims=True)
    group = jnp.where(chosen == expert.astype(f32), 0.0, 1.0)
    lane_i = lax.broadcasted_iota(jnp.int32, (token_count, token_count), 1)
    row_i = lax.broadcasted_iota(jnp.int32, (token_count, token_count), 0)
    lane = lane_i.astype(f32)
    groups = jnp.where(lane == group, has_route, 0.0)
    before = jnp.where(lane_i < row_i, 1.0, 0.0)
    ranks = jnp.dot(before.astype(bf16), groups.astype(bf16), preferred_element_type=f32)
    rank = jnp.sum(ranks * groups, axis=-1, keepdims=True)
    placing = jnp.where(lane == group * half + rank, has_route, 0.0).astype(bf16)
    place_s[...] = placing
    for c in range(CHUNKS):
        cols = slice(c * piece, (c + 1) * piece)
        normed = (tok_ref[:, cols].astype(f32) * inverse).astype(bf16)
        packed = lax.dot_general(
            placing, normed, (((0,), (0,)), ((), ())), preferred_element_type=f32
        ).astype(bf16)
        xbuf[0, 0:half, cols] = packed[:half]
        other[:, cols] = packed[half:]

    pl.semaphore_wait(barrier, 11)
    c0.start()
    c1.start()
    c2.start()
    seg_copies = []
    for k in range(1, 8):
        copy = pltpu.make_async_remote_copy(
            src_ref=segrow_ref, dst_ref=segs.at[k - 1],
            send_sem=seg_send.at[k - 1], recv_sem=seg_recv.at[k - 1],
            device_id=(section, lax.rem(me + k, count)), device_id_type=MESH,
        )
        copy.start()
        seg_copies.append(copy)

    def expert_rows(q):
        def step(j, carry):
            both = jnp.dot(xbuf[q], wgu[j], preferred_element_type=f32)
            gate, up = both[:, :128], both[:, 128:]
            act[j] = (gate / (1.0 + jnp.exp(-gate)) * up).astype(bf16)
            return carry

        lax.fori_loop(0, hidden_parts, step, 0)
        return jnp.concatenate([act[j] for j in range(hidden_parts)], axis=-1)

    def down(rows, c):
        return jnp.dot(
            rows, wd[:, c * piece : (c + 1) * piece], preferred_element_type=f32
        )

    c1.wait_recv()
    c5.start()
    c0.wait_recv()
    c3.start()
    c4.start()
    for load in loads:
        load.wait()
    rows = expert_rows(0)
    for c in range(CHUNKS):
        own[c] = down(rows, c)
    c2.wait_recv()
    c4.wait_recv()
    c6.start()
    rows = expert_rows(2)
    for c in range(CHUNKS):
        pz[c] = down(rows, c).astype(bf16)
        if c < 2:
            to_z[c].start()
    c3.wait_recv()
    rows = expert_rows(1)
    for c in (2, 3, 0, 1):
        py[c] = down(rows, c).astype(bf16)
        if c >= 2:
            to_y[c].start()
    c5.wait_recv()
    c6.wait_recv()
    rows = expert_rows(3)
    for c in (0, 2, 1, 3):
        pd[c] = down(rows, c).astype(bf16)
        first_hop[c].start()
    for c in (0, 2, 1, 3):
        first_hop[c].wait_recv()
        if c < 2:
            py[c] = (py[c].astype(f32) + r1[c].astype(f32)).astype(bf16)
            to_y[c].start()
        else:
            pz[c] = (pz[c].astype(f32) + r1[c].astype(f32)).astype(bf16)
            to_z[c].start()
    weights.start()
    order = (0, 2, 1, 3)
    for c in order:
        to_y[c].wait_recv()
        to_z[c].wait_recv()
        total = own[c] + r2y[c].astype(f32) + r2z[c].astype(f32)
        own[c] = total
        sm[c] = total[half:].astype(bf16)
        to_mirror[c].start()

    def onward(c):
        return pltpu.make_async_remote_copy(
            src_ref=lo.at[c], dst_ref=lbuf.at[z], send_sem=l_send.at[c], recv_sem=l_recv.at[z],
            device_id=(following, c * 2 + y), device_id_type=MESH,
        )

    squares = jnp.zeros((token_count, 1), f32)
    for c in order:
        to_mirror[c].wait_recv()
        merged = jnp.concatenate([own[c][:half].astype(bf16), rm[c]], axis=0)
        spread = jnp.dot(place_s[...], merged, preferred_element_type=f32)
        cols = slice(c * piece, (c + 1) * piece)
        result = (tok_ref[:, cols].astype(f32) + weight * spread).astype(bf16)
        lo[c] = result
        onward(c).start()
        lo_ref[:, cols] = result
        wide = result.astype(f32)
        squares += jnp.sum(wide * wide, axis=-1, keepdims=True)
    scale_out[...] = jnp.broadcast_to(
        lax.rsqrt(squares / width + EPSILON), scale_out.shape
    )
    scale_copy = pltpu.make_async_remote_copy(
        src_ref=scale_out, dst_ref=scale_in, send_sem=send_sem.at[24], recv_sem=recv_sem.at[24],
        device_id=(following, me), device_id_type=MESH,
    )
    scale_copy.start()

    for copy in seg_copies:
        copy.wait_recv()
    mine = segcol_ref[...]
    start = jnp.sum(
        jnp.where(segrow_ref[...] < mine, 1.0, 0.0), axis=-1, keepdims=True
    )
    for k in range(7):
        start += jnp.sum(jnp.where(segs[k] < mine, 1.0, 0.0), axis=-1, keepdims=True)
    index = (
        lax.broadcasted_iota(jnp.int32, (token_count, 1), 0) + me * token_count
    ).astype(f32)
    angles = (index - start) * freq_ref[...]
    head_dim = gq_ref.shape[-1]
    cosine = jnp.cos(angles)
    lanes = lax.broadcasted_iota(jnp.int32, (token_count, head_dim), 1)
    sine = jnp.where(lanes < head_dim // 2, -1.0, 1.0) * jnp.sin(angles)

    weights_in.wait_recv()

    def project(rows):
        result = jnp.dot(rows[:, : piece // 2], wbuf[0], preferred_element_type=f32)
        result += jnp.dot(rows[:, piece // 2 :], wbuf[1], preferred_element_type=f32)
        return result.astype(bf16)

    def arrival(source):
        return pltpu.make_async_remote_copy(
            src_ref=lo.at[0], dst_ref=lbuf.at[source], send_sem=l_send.at[0],
            recv_sem=l_recv.at[source], device_id=(preceding, source * 2 + y),
            device_id_type=MESH,
        )

    def partial_copy(k):
        target = lax.rem(z + k, 4)
        return pltpu.make_async_remote_copy(
            src_ref=lbuf_out(k), dst_ref=rbuf.at[k - 1], send_sem=p_send.at[k - 1],
            recv_sem=p_recv.at[k - 1], device_id=(section, target * 2 + y), device_id_type=MESH,
        )

    def lbuf_out(k):
        return rbuf.at[2 + k]

    for k in (2, 1, 3):
        source = lax.rem(z + k, 4)
        arrival(source).wait_recv()
        rbuf[2 + k] = project(lbuf[source])
        partial_copy(k).start()
    arrival(z).wait_recv()
    mixed = project(lbuf[z]).astype(f32)
    scale_copy.wait_recv()
    for k in range(1, 4):
        partial_copy(k).wait_recv()
        mixed += rbuf[k - 1].astype(f32)
    mixed *= scale_in[:, 0:1]

    def turn(values, gain):
        values = values * lax.rsqrt(jnp.mean(values * values, axis=-1, keepdims=True) + EPSILON)
        values = values * gain
        return values * cosine + pltpu.roll(values, head_dim // 2, 1) * sine

    key = turn(mixed[:, query_width : query_width + head_dim], gk_ref[...]).astype(bf16)
    kv[0, :, 0:head_dim] = key
    kv[0, :, head_dim:] = mixed[:, query_width + head_dim :].astype(bf16)
    reach = kv.shape[0] - 1
    kv_copies = []
    for k in range(1, reach + 1):
        copy = pltpu.make_async_remote_copy(
            src_ref=kv.at[0], dst_ref=kv.at[k], send_sem=kv_send.at[k - 1],
            recv_sem=kv_recv.at[k - 1], device_id=(section, lax.rem(me + k, count)),
            device_id_type=MESH,
        )
        copy.start()
        kv_copies.append(copy)
    queries = [
        turn(mixed[:, h * head_dim : (h + 1) * head_dim], gq_ref[...]).astype(bf16)
        for h in range(query_width // head_dim)
    ]
    for copy in kv_copies:
        copy.wait_recv()
    key_count = (reach + 1) * token_count
    place = lax.broadcasted_iota(jnp.int32, (1, key_count), 1)
    slot = place // token_count
    key_index = (lax.rem(me - slot + count, count) * token_count + place % token_count).astype(f32)
    allowed = (key_index <= index) & (key_index >= start)
    everything = kv[...].reshape(key_count, 2 * head_dim)
    keys, values = everything[:, :head_dim], everything[:, head_dim:]
    for h, query in enumerate(queries):
        scores = lax.dot_general(
            query, keys, (((1,), (1,)), ((), ())), preferred_element_type=f32
        ) * (1.0 / math.sqrt(head_dim))
        probs = jnp.where(allowed, jnp.exp(scores), 0.0)
        mass = jnp.sum(probs, axis=-1, keepdims=True)
        out = jnp.dot(probs.astype(bf16), values, preferred_element_type=f32) / mass
        att_ref[:, h * head_dim : (h + 1) * head_dim] = out.astype(bf16)

    for copy in [c0, c1, c2, c3, c4, c5, c6, weights, scale_copy]:
        copy.wait_send()
    for copy in first_hop + to_y + to_z + to_mirror + seg_copies + kv_copies:
        copy.wait_send()
    for c in range(CHUNKS):
        onward(c).wait_send()
    for k in range(1, 4):
        partial_copy(k).wait_send()


def fused_on_device(
    tokens, routes, router_weights, w_gate, w_up, w_down, w_query, w_keyval,
    gain_query, gain_key, segment_ids,
):
    token_count, width = tokens.shape[1:]
    half = token_count // 2
    piece = width // CHUNKS
    hidden = w_gate.shape[-1]
    head_dim = gain_query.shape[-1]
    out_width = w_query.shape[-1] + w_keyval.shape[-1]
    reach = (SEG_MOST - 1) // token_count + 1
    half_count = head_dim // 2
    frequency = ROPE_BASE ** (-(jnp.arange(half_count, dtype=jnp.float32) * 2.0) / head_dim)
    frequency = jnp.concatenate([frequency, frequency])[None]
    bf16, f32 = jnp.bfloat16, jnp.float32
    vmem, hbm = pl.BlockSpec(memory_space=pltpu.VMEM), pl.BlockSpec(memory_space=pl.ANY)
    chunked = (CHUNKS, token_count, piece)
    dma = pltpu.SemaphoreType.DMA
    layer_out, attended = pl.pallas_call(
        fused_kernel,
        out_shape=(
            jax.ShapeDtypeStruct((token_count, width), bf16),
            jax.ShapeDtypeStruct((token_count, w_query.shape[-1]), bf16),
        ),
        in_specs=[vmem] * 3 + [hbm] * 5 + [vmem] * 5,
        out_specs=(vmem, vmem),
        scratch_shapes=[
            pltpu.VMEM((4, token_count, width), bf16),
            pltpu.VMEM((half, width), bf16),
            pltpu.VMEM((hidden // 128, width, 256), bf16),
            pltpu.VMEM((hidden, width), bf16),
            pltpu.VMEM((hidden // 128, token_count, 128), bf16),
            pltpu.VMEM(chunked, bf16),
            pltpu.VMEM(chunked, bf16),
            pltpu.VMEM(chunked, bf16),
            pltpu.VMEM(chunked, f32),
            pltpu.VMEM(chunked, bf16),
            pltpu.VMEM(chunked, bf16),
            pltpu.VMEM(chunked, bf16),
            pltpu.VMEM((CHUNKS, half, piece), bf16),
            pltpu.VMEM((CHUNKS, half, piece), bf16),
            pltpu.VMEM(chunked, bf16),
            pltpu.VMEM(chunked, bf16),
            pltpu.VMEM((2, w_query.shape[1], out_width), bf16),
            pltpu.VMEM((6, token_count, out_width), bf16),
            pltpu.VMEM((token_count, 128), f32),
            pltpu.VMEM((token_count, 128), f32),
            pltpu.VMEM((reach + 1, token_count, 2 * head_dim), bf16),
            pltpu.VMEM((7, 1, token_count), jnp.int32),
            pltpu.VMEM((token_count, token_count), bf16),
            dma((16,)),
            dma((25,)), dma((25,)),
            dma((4,)), dma((4,)),
            dma((3,)), dma((3,)),
            dma((reach,)), dma((reach,)),
            dma((7,)), dma((7,)),
        ],
        compiler_params=pltpu.CompilerParams(
            collective_id=0, has_side_effects=True, vmem_limit_bytes=56 * 1024 * 1024
        ),
    )(
        tokens[0], routes[0], router_weights[0], w_gate[0, 0], w_up[0, 0], w_down[0, 0],
        w_query[0], w_keyval[0], gain_query, gain_key, segment_ids,
        segment_ids.reshape(token_count, 1), frequency,
    )
    return (layer_out[None], attended[None])


def solution(mesh):
    in_specs = (
        P("section", "ep", None),
        P("section", "ep", None),
        P("section", "ep", None),
        P("section", "ep", None, None),
        P("section", "ep", None, None),
        P("section", "ep", None, None),
        P("section", "ep", None),
        P("section", "ep", None),
        P("section", None),
        P("section", None),
        P("section", "ep"),
    )
    out_specs = (P("section", "ep", None), P("section", "ep", None))
    return jax.shard_map(
        fused_on_device if mesh.shape["ep"] == 8 else on_device, mesh=mesh, in_specs=in_specs, out_specs=out_specs, check_vma=False
    )
```

```python
import math

import jax
import jax.numpy as jnp
from jax import lax
from jax.experimental import pallas as pl
from jax.experimental.pallas import tpu as pltpu
from jax.sharding import PartitionSpec as P

OWNERS = 4
SEG_MOST = 512


EPSILON = 1e-06
ROPE_BASE = 1000000.0
FAR_INDEX = 1073741824


def passed_along(block, axis, distance):
    devices = range(lax.axis_size(axis))
    route = [((i - distance) % len(devices), i) for i in devices]
    return lax.ppermute(block, axis, route)


def prefix(shard, axis, combine, identity):
    length, mine = (lax.axis_size(axis), lax.axis_index(axis))
    everything = jax.tree.map(lambda part: lax.all_gather(part, axis), shard)
    start = jax.tree.map(
        lambda part, zero: jnp.broadcast_to(jnp.asarray(zero, part.dtype), part.shape),
        shard,
        identity,
    )

    def step(k, before):
        reached = k < mine
        new = combine(before, jax.tree.map(lambda part: part[k], everything))
        return jax.tree.map(lambda a, b: jnp.where(reached, a, b), new, before)

    return lax.fori_loop(0, length, step, start)


def passed_along_2(value, axis, steps):
    count = lax.axis_size(axis)
    leading, last = (max(0, -steps), min(count, count - steps))
    return lax.ppermute(value, axis, [(source, source + steps) for source in range(leading, last)])


def rms_rows(values):
    return values * lax.rsqrt(jnp.mean(values * values, axis=-1, keepdims=True) + EPSILON)


def rotary(values, position):
    half_count = values.shape[-1] // 2
    frequency = ROPE_BASE ** (-(jnp.arange(half_count, dtype=jnp.float32) * 2.0) / values.shape[-1])
    angles = position.astype(jnp.float32)[:, None] * frequency[None, :]
    cosine = jnp.concatenate([jnp.cos(angles), jnp.cos(angles)], axis=-1)[:, None, :]
    sine = jnp.concatenate([jnp.sin(angles), jnp.sin(angles)], axis=-1)[:, None, :]
    turned = jnp.concatenate([-values[..., half_count:], values[..., :half_count]], axis=-1)
    return values * cosine + turned * sine


def feed_forward(row_block, gate_part, up_part, down_part):
    gate_proj = jnp.dot(row_block, gate_part, preferred_element_type=jnp.float32)
    up_proj = jnp.dot(row_block, up_part, preferred_element_type=jnp.float32)
    activated = (jax.nn.silu(gate_proj) * up_proj).astype(jnp.bfloat16)
    return jnp.dot(activated, down_part, preferred_element_type=jnp.float32)


def keep_later(earlier, later):
    same_id = earlier[0] == later[0]
    newer_id = later[0] > earlier[0]
    start_at = jnp.where(
        same_id, jnp.minimum(earlier[1], later[1]), jnp.where(newer_id, later[1], earlier[1])
    )
    return (jnp.maximum(earlier[0], later[0]), start_at)


def on_device(
    tokens,
    routes,
    router_weights,
    w_gate,
    w_up,
    w_down,
    w_query,
    w_keyval,
    gain_query,
    gain_key,
    segment_ids,
):
    device_count = lax.axis_size("ep")
    expert_count = device_count // OWNERS
    token_count = tokens.shape[1]
    model_width = tokens.shape[2]
    capacity = OWNERS * max(1, token_count // device_count)
    wide_tokens = tokens[0].astype(jnp.float32)
    normed = rms_rows(wide_tokens).astype(jnp.bfloat16)
    inside = routes[0] < expert_count
    has_route = jnp.any(inside, axis=-1)
    chosen = jnp.sum(jnp.where(inside, routes[0], 0), axis=-1)
    weight_kept = jnp.sum(jnp.where(inside, router_weights[0], 0.0), axis=-1)
    expert_ids = jnp.arange(expert_count, dtype=jnp.int32)
    member = ((chosen[:, None] == expert_ids[None, :]) & has_route[:, None]).astype(jnp.int32)
    token_ids = jnp.arange(token_count, dtype=jnp.int32)
    earlier = (token_ids[None, :] < token_ids[:, None]).astype(jnp.float32)
    ranks = jnp.dot(earlier, member.astype(jnp.float32)).astype(jnp.int32)
    rank_within = jnp.sum(ranks * member, axis=-1)
    slot_index = jnp.where(has_route, chosen * capacity + rank_within, -1)
    slot_ids = jnp.arange(expert_count * capacity, dtype=jnp.int32)
    placing = (slot_ids[:, None] == slot_index[None, :]).astype(jnp.bfloat16)
    packed = jnp.dot(placing, normed, preferred_element_type=jnp.float32).astype(jnp.bfloat16)
    gate_part = w_gate[0, 0]
    up_part = w_up[0, 0]
    down_part = w_down[0, 0]
    spread = jnp.broadcast_to(
        packed.reshape(expert_count, 1, capacity, model_width),
        (expert_count, OWNERS, capacity, model_width),
    ).reshape(device_count, capacity, model_width)
    received = lax.all_to_all(spread, "ep", split_axis=0, concat_axis=0, tiled=True)
    partial_out = feed_forward(
        received.reshape(-1, model_width), gate_part, up_part, down_part
    ).reshape(received.shape)
    returned_rows = lax.all_to_all(
        partial_out.astype(jnp.bfloat16), "ep", split_axis=0, concat_axis=0, tiled=True
    ).astype(partial_out.dtype)
    merged = jnp.sum(
        returned_rows.reshape(expert_count, OWNERS, capacity, model_width), axis=1
    ).reshape(expert_count * capacity, model_width)
    fetched_rows = jnp.take(merged, jnp.maximum(slot_index, 0), axis=0)
    expert_out = jnp.where(has_route[:, None], fetched_rows, 0.0)
    layer_out = (wide_tokens + weight_kept[:, None] * expert_out).astype(jnp.bfloat16)
    arrived = passed_along(layer_out, "section", 1)
    lifted = rms_rows(arrived.astype(jnp.float32)).astype(jnp.bfloat16)
    head_dim = gain_query.shape[-1]
    query_width = w_query.shape[-1]
    head_count = query_width // head_dim
    query_raw = jnp.dot(
        lifted,
        lax.all_gather(w_query[0], "ep", axis=0, tiled=True),
        preferred_element_type=jnp.float32,
    )
    keyval_raw = jnp.dot(
        lifted,
        lax.all_gather(w_keyval[0], "ep", axis=0, tiled=True),
        preferred_element_type=jnp.float32,
    )
    segment_row = segment_ids[0]
    first_index = lax.axis_index("ep") * token_count
    global_index = first_index + jnp.arange(token_count, dtype=jnp.int32)
    local_start = jnp.min(
        jnp.where(
            segment_row[None, :] == segment_row[:, None], global_index[None, :], FAR_INDEX
        ),
        axis=1,
    )
    empty_prior = (jnp.full((1,), -1, jnp.int32), jnp.full((1,), FAR_INDEX, jnp.int32))
    prior_id, prior_start = prefix(
        (segment_row[-1:], local_start[-1:]), "ep", keep_later, empty_prior
    )
    start_index = jnp.where(segment_row == prior_id[0], prior_start[0], local_start).astype(
        jnp.int32
    )
    position = global_index - start_index
    query = rotary(
        rms_rows(query_raw.reshape(token_count, head_count, head_dim)) * gain_query[0], position
    ).astype(jnp.bfloat16)
    key_part = rotary(rms_rows(keyval_raw[:, None, :head_dim]) * gain_key[0], position)[
        :, 0
    ].astype(jnp.bfloat16)
    value_part = keyval_raw[:, head_dim:].astype(jnp.bfloat16)
    key_value = jnp.concatenate([key_part, value_part], axis=-1)
    reach = (SEG_MOST - 1) // token_count + 1
    earlier_pieces = []
    for distance in range(1, reach + 1):
        earlier_pieces.append(passed_along_2(key_value, "ep", distance))
    window = jnp.concatenate(earlier_pieces[::-1] + [key_value], axis=0)
    key_index = (
        first_index - reach * token_count + jnp.arange((reach + 1) * token_count, dtype=jnp.int32)
    )
    query_rows = query.reshape(token_count * head_count, head_dim)
    query_index = jnp.repeat(global_index, head_count)
    query_start = jnp.repeat(start_index, head_count)
    score_scale = 1.0 / math.sqrt(head_dim)
    scores = (
        jnp.einsum(
            "qd,kd->qk", query_rows, window[:, :head_dim], preferred_element_type=jnp.float32
        )
        * score_scale
    )
    allowed = (key_index[None, :] <= query_index[:, None]) & (
        key_index[None, :] >= query_start[:, None]
    )
    probabilities = jnp.where(allowed, jnp.exp(scores), 0.0)
    total_mass = jnp.sum(probabilities, axis=-1)
    mixed = jnp.dot(
        probabilities.astype(jnp.bfloat16), window[:, head_dim:], preferred_element_type=jnp.float32
    )
    attended = (mixed / total_mass[:, None]).astype(jnp.bfloat16).reshape(token_count, query_width)
    return (layer_out[None], attended[None])


MESH = pl.DeviceIdType.MESH
CHUNKS = 4


def fused_kernel(
    tok_ref, route_ref, rw_ref, wg_hbm, wu_hbm, wd_hbm, wq_hbm, wkv_hbm,
    gq_ref, gk_ref, segrow_ref, freq_ref,
    lo_ref, att_ref,
    xbuf, other, wgu, wd, act, pd, py, pz, own, r1, r2y, r2z, sm, rm,
    lo, lbuf, wbuf, rbuf, scale_out, scale_in, kv, segs, place_s,
    load_sem, send_sem, recv_sem, l_send, l_recv, p_send, p_recv,
    kv_send, kv_recv, seg_send, seg_recv,
):
    f32, bf16 = jnp.float32, jnp.bfloat16
    section = lax.axis_index("section")
    sections = lax.axis_size("section")
    me = lax.axis_index("ep")
    count = lax.axis_size("ep")
    z, y = me // 2, me % 2
    expert = z // 2
    token_count, width = tok_ref.shape
    half = token_count // 2
    piece = width // CHUNKS
    y_peer = z * 2 + (1 - y)
    z_peer = (z // 2 * 2 + 1 - z % 2) * 2 + y
    mirror = lax.rem(z + 2, 4) * 2 + y
    following = lax.rem(section + 1, sections)
    preceding = lax.rem(section + sections - 1, sections)

    barrier = pltpu.get_barrier_semaphore()
    for k in range(1, 8):
        pl.semaphore_signal(
            barrier, inc=1, device_id=(section, lax.rem(me + k, count)), device_id_type=MESH
        )
    for k in range(4):
        pl.semaphore_signal(barrier, inc=1, device_id=(preceding, k * 2 + y), device_id_type=MESH)

    hidden_parts = wgu.shape[0]
    loads = []
    for j in range(hidden_parts):
        cols = pl.ds(j * 128, 128)
        loads.append((wg_hbm.at[:, cols], wgu.at[j, :, pl.ds(0, 128)]))
        loads.append((wu_hbm.at[:, cols], wgu.at[j, :, pl.ds(128, 128)]))
    loads.append((wd_hbm, wd))
    query_width = wq_hbm.shape[1]
    loads.append((wq_hbm, wbuf.at[y, :, pl.ds(0, query_width)]))
    loads.append((wkv_hbm, wbuf.at[y, :, pl.ds(query_width, wkv_hbm.shape[1])]))
    loads = [
        pltpu.make_async_copy(src, dst, load_sem.at[i]) for i, (src, dst) in enumerate(loads)
    ]
    for load in loads:
        load.start()

    def remote(src, dst, i, target):
        return pltpu.make_async_remote_copy(
            src_ref=src, dst_ref=dst, send_sem=send_sem.at[i], recv_sem=recv_sem.at[i],
            device_id=(section, target), device_id_type=MESH,
        )

    low, high = pl.ds(0, half), pl.ds(half, half)
    blocks = [pl.ds(b * (half // 4), half // 4) for b in range(4)]
    upper = [pl.ds(half + b * (half // 4), half // 4) for b in range(4)]
    c0 = [
        remote(other.at[s], xbuf.at[0, u], 27 + b, mirror)
        for b, (s, u) in enumerate(zip(blocks, upper))
    ]
    c1 = remote(xbuf.at[0, low], xbuf.at[1, low], 1, y_peer)
    c2 = remote(xbuf.at[0, low], xbuf.at[2, low], 2, z_peer)
    c3 = [remote(xbuf.at[0, u], xbuf.at[1, u], 31 + b, y_peer) for b, u in enumerate(upper)]
    c4 = [remote(xbuf.at[0, u], xbuf.at[2, u], 35 + b, z_peer) for b, u in enumerate(upper)]
    c5 = remote(xbuf.at[1, low], xbuf.at[3, low], 5, z_peer)
    c6 = [remote(xbuf.at[2, u], xbuf.at[3, u], 39 + b, y_peer) for b, u in enumerate(upper)]
    def parts(src, dst, base, target):
        return {
            (c, h): remote(
                src.at[c, pl.ds(h * half, half)], dst.at[c, pl.ds(h * half, half)],
                base + 2 * c + h, target(c),
            )
            for c in range(CHUNKS) for h in range(2)
        }

    first_hop = parts(pd, r1, 43, lambda c: z_peer if c < 2 else y_peer)
    to_y = parts(py, r2y, 51, lambda c: y_peer)
    to_z = parts(pz, r2z, 59, lambda c: z_peer)
    to_mirror = [remote(sm.at[c], rm.at[c], 19 + c, mirror) for c in range(CHUNKS)]
    weights = remote(wbuf.at[y], wbuf.at[y], 23, y_peer)
    weights_in = remote(wbuf.at[1 - y], wbuf.at[1 - y], 23, y_peer)

    squares = jnp.zeros((token_count, 1), f32)
    for c in range(CHUNKS):
        part = tok_ref[:, c * piece : (c + 1) * piece].astype(f32)
        squares += jnp.sum(part * part, axis=-1, keepdims=True)
    inverse = lax.rsqrt(squares / width + EPSILON)
    lane_i = lax.broadcasted_iota(jnp.int32, (token_count, token_count), 1)
    row_i = lax.broadcasted_iota(jnp.int32, (token_count, token_count), 0)

    def column(row):
        return jnp.sum(jnp.where(lane_i == row_i, row, 0.0), axis=-1, keepdims=True)

    routes = route_ref[...]
    inside = routes < 2
    has_route = column(jnp.sum(jnp.where(inside, 1.0, 0.0), axis=0, keepdims=True))
    chosen = column(
        jnp.sum(jnp.where(inside, routes.astype(f32), 0.0), axis=0, keepdims=True)
    )
    weight = column(jnp.sum(jnp.where(inside, rw_ref[...], 0.0), axis=0, keepdims=True))
    group = jnp.where(chosen == expert.astype(f32), 0.0, 1.0)
    lane = lane_i.astype(f32)
    groups = jnp.where(lane == group, has_route, 0.0)
    before = jnp.where(lane_i < row_i, 1.0, 0.0)
    ranks = jnp.dot(before.astype(bf16), groups.astype(bf16), preferred_element_type=f32)
    rank = jnp.sum(ranks * groups, axis=-1, keepdims=True)
    placing = jnp.where(lane == group * half + rank, has_route, 0.0).astype(bf16)
    place_s[...] = placing
    for c in range(CHUNKS):
        cols = slice(c * piece, (c + 1) * piece)
        normed = (tok_ref[:, cols].astype(f32) * inverse).astype(bf16)
        packed = lax.dot_general(
            placing, normed, (((0,), (0,)), ((), ())), preferred_element_type=f32
        ).astype(bf16)
        xbuf[0, 0:half, cols] = packed[:half]
        other[:, cols] = packed[half:]

    pl.semaphore_wait(barrier, 11)
    for copy in c0:
        copy.start()
    c1.start()
    c2.start()
    seg_copies = []
    for k in range(1, 8):
        copy = pltpu.make_async_remote_copy(
            src_ref=segrow_ref, dst_ref=segs.at[k - 1],
            send_sem=seg_send.at[k - 1], recv_sem=seg_recv.at[k - 1],
            device_id=(section, lax.rem(me + k, count)), device_id_type=MESH,
        )
        copy.start()
        seg_copies.append(copy)

    def expert_rows(q):
        def step(j, carry):
            both = jnp.dot(xbuf[q], wgu[j], preferred_element_type=f32)
            gate, up = both[:, :128], both[:, 128:]
            act[j] = (gate / (1.0 + jnp.exp(-gate)) * up).astype(bf16)
            return carry

        lax.fori_loop(0, hidden_parts, step, 0)
        return jnp.concatenate([act[j] for j in range(hidden_parts)], axis=-1)

    def down(rows, c):
        return jnp.dot(
            rows, wd[:, c * piece : (c + 1) * piece], preferred_element_type=f32
        )

    for b in range(4):
        c0[b].wait_recv()
        c3[b].start()
        c4[b].start()
        if b == 1:
            c1.wait_recv()
            c5.start()
    for b in range(4):
        c4[b].wait_recv()
        c6[b].start()
    for load in loads:
        load.wait()
    rows = expert_rows(0)
    for c in range(CHUNKS):
        own[c] = down(rows, c)
    c2.wait_recv()
    rows = expert_rows(2)
    for c in range(CHUNKS):
        pz[c] = down(rows, c).astype(bf16)
        if c < 2:
            to_z[c, 1].start()
    for copy in c3:
        copy.wait_recv()
    rows = expert_rows(1)
    for c in (2, 3, 0, 1):
        py[c] = down(rows, c).astype(bf16)
        if c >= 2:
            to_y[c, 1].start()
    c5.wait_recv()
    for copy in c6:
        copy.wait_recv()
    rows = expert_rows(3)
    order = (0, 2, 1, 3)
    for c in order:
        pd[c] = down(rows, c).astype(bf16)
        first_hop[c, 1].start()
    for c in order:
        first_hop[c, 0].start()
    for c in order:
        (to_z if c < 2 else to_y)[c, 0].start()
    for h in (1, 0):
        part = slice(h * half, (h + 1) * half)
        for c in order:
            first_hop[c, h].wait_recv()
            out, copies = (py, to_y) if c < 2 else (pz, to_z)
            out[c, part] = (out[c, part].astype(f32) + r1[c, part].astype(f32)).astype(bf16)
            copies[c, h].start()
    weights.start()
    for h in (1, 0):
        part = slice(h * half, (h + 1) * half)
        for c in order:
            to_y[c, h].wait_recv()
            to_z[c, h].wait_recv()
            total = own[c, part] + r2y[c, part].astype(f32) + r2z[c, part].astype(f32)
            if h:
                sm[c] = total.astype(bf16)
                to_mirror[c].start()
            else:
                own[c, part] = total

    def onward(c):
        return pltpu.make_async_remote_copy(
            src_ref=lo.at[c], dst_ref=lbuf.at[z], send_sem=l_send.at[c], recv_sem=l_recv.at[z],
            device_id=(following, c * 2 + y), device_id_type=MESH,
        )

    squares = jnp.zeros((token_count, 1), f32)
    for c in order:
        to_mirror[c].wait_recv()
        merged = jnp.concatenate([own[c][:half].astype(bf16), rm[c]], axis=0)
        spread = jnp.dot(place_s[...], merged, preferred_element_type=f32)
        cols = slice(c * piece, (c + 1) * piece)
        result = (tok_ref[:, cols].astype(f32) + weight * spread).astype(bf16)
        lo[c] = result
        onward(c).start()
        lo_ref[:, cols] = result
        wide = result.astype(f32)
        squares += jnp.sum(wide * wide, axis=-1, keepdims=True)
    scale_out[...] = jnp.broadcast_to(
        lax.rsqrt(squares / width + EPSILON), scale_out.shape
    )
    scale_copy = pltpu.make_async_remote_copy(
        src_ref=scale_out, dst_ref=scale_in, send_sem=send_sem.at[24], recv_sem=recv_sem.at[24],
        device_id=(following, me), device_id_type=MESH,
    )
    scale_copy.start()

    for copy in seg_copies:
        copy.wait_recv()
    own_row = segrow_ref[...].astype(f32)
    mine = column(own_row)
    start = jnp.sum(jnp.where(own_row < mine, 1.0, 0.0), axis=-1, keepdims=True)
    for k in range(7):
        start += jnp.sum(jnp.where(segs[k].astype(f32) < mine, 1.0, 0.0), axis=-1, keepdims=True)
    index = (
        lax.broadcasted_iota(jnp.int32, (token_count, 1), 0) + me * token_count
    ).astype(f32)
    angles = (index - start) * freq_ref[...]
    head_dim = gq_ref.shape[-1]
    cosine = jnp.cos(angles)
    lanes = lax.broadcasted_iota(jnp.int32, (token_count, head_dim), 1)
    sine = jnp.where(lanes < head_dim // 2, -1.0, 1.0) * jnp.sin(angles)

    weights_in.wait_recv()

    def project(rows):
        result = jnp.dot(rows[:, : piece // 2], wbuf[0], preferred_element_type=f32)
        result += jnp.dot(rows[:, piece // 2 :], wbuf[1], preferred_element_type=f32)
        return result

    def arrival(source):
        return pltpu.make_async_remote_copy(
            src_ref=lo.at[0], dst_ref=lbuf.at[source], send_sem=l_send.at[0],
            recv_sem=l_recv.at[source], device_id=(preceding, source * 2 + y),
            device_id_type=MESH,
        )

    z_side = z // 2 * 2 + 1 - z % 2

    def partial_copy(slot, target):
        return pltpu.make_async_remote_copy(
            src_ref=rbuf.at[3 + slot], dst_ref=rbuf.at[slot], send_sem=p_send.at[slot],
            recv_sem=p_recv.at[slot], device_id=(section, target), device_id_type=MESH,
        )

    partial_copies = [
        partial_copy(0, z_peer), partial_copy(1, z_peer), partial_copy(2, mirror)
    ]
    source = lax.rem(z_side + 2, 4)
    arrival(source).wait_recv()
    rbuf[4] = project(lbuf[source]).astype(bf16)
    partial_copies[1].start()
    source = lax.rem(z + 2, 4)
    arrival(source).wait_recv()
    crossing = project(lbuf[source])
    arrival(z_side).wait_recv()
    rbuf[3] = project(lbuf[z_side]).astype(bf16)
    partial_copies[0].start()
    partial_copies[1].wait_recv()
    rbuf[5] = (crossing + rbuf[1].astype(f32)).astype(bf16)
    partial_copies[2].start()
    arrival(z).wait_recv()
    mixed = project(lbuf[z])
    scale_copy.wait_recv()
    partial_copies[0].wait_recv()
    mixed += rbuf[0].astype(f32)
    partial_copies[2].wait_recv()
    mixed += rbuf[2].astype(f32)
    mixed *= scale_in[:, 0:1]

    def turn(values, gain):
        values = values * lax.rsqrt(jnp.mean(values * values, axis=-1, keepdims=True) + EPSILON)
        values = values * gain
        return values * cosine + pltpu.roll(values, head_dim // 2, 1) * sine

    key = turn(mixed[:, query_width : query_width + head_dim], gk_ref[...]).astype(bf16)
    kv[0, :, 0:head_dim] = key
    kv[0, :, head_dim:] = mixed[:, query_width + head_dim :].astype(bf16)
    reach = kv.shape[0] - 1
    kv_copies = []
    for k in range(1, reach + 1):
        copy = pltpu.make_async_remote_copy(
            src_ref=kv.at[0], dst_ref=kv.at[k], send_sem=kv_send.at[k - 1],
            recv_sem=kv_recv.at[k - 1], device_id=(section, lax.rem(me + k, count)),
            device_id_type=MESH,
        )
        copy.start()
        kv_copies.append(copy)
    queries = [
        turn(mixed[:, h * head_dim : (h + 1) * head_dim], gq_ref[...]).astype(bf16)
        for h in range(query_width // head_dim)
    ]
    for copy in kv_copies:
        copy.wait_recv()
    key_count = (reach + 1) * token_count
    place = lax.broadcasted_iota(jnp.int32, (1, key_count), 1)
    slot = place // token_count
    key_index = (lax.rem(me - slot + count, count) * token_count + place % token_count).astype(f32)
    allowed = (key_index <= index) & (key_index >= start)
    everything = kv[...].reshape(key_count, 2 * head_dim)
    keys, values = everything[:, :head_dim], everything[:, head_dim:]
    for h, query in enumerate(queries):
        scores = lax.dot_general(
            query, keys, (((1,), (1,)), ((), ())), preferred_element_type=f32
        ) * (1.0 / math.sqrt(head_dim))
        probs = jnp.where(allowed, jnp.exp(scores), 0.0)
        mass = jnp.sum(probs, axis=-1, keepdims=True)
        out = jnp.dot(probs.astype(bf16), values, preferred_element_type=f32) / mass
        att_ref[:, h * head_dim : (h + 1) * head_dim] = out.astype(bf16)

    for copy in [c1, c2, c5, weights, scale_copy, *c0, *c3, *c4, *c6]:
        copy.wait_send()
    for copies in (first_hop, to_y, to_z):
        for copy in copies.values():
            copy.wait_send()
    for copy in to_mirror + seg_copies + kv_copies + partial_copies:
        copy.wait_send()
    for c in range(CHUNKS):
        onward(c).wait_send()


def fused_on_device(
    tokens, routes, router_weights, w_gate, w_up, w_down, w_query, w_keyval,
    gain_query, gain_key, segment_ids,
):
    token_count, width = tokens.shape[1:]
    half = token_count // 2
    piece = width // CHUNKS
    hidden = w_gate.shape[-1]
    head_dim = gain_query.shape[-1]
    out_width = w_query.shape[-1] + w_keyval.shape[-1]
    reach = (SEG_MOST - 1) // token_count + 1
    half_count = head_dim // 2
    frequency = ROPE_BASE ** (-(jnp.arange(half_count, dtype=jnp.float32) * 2.0) / head_dim)
    frequency = jnp.concatenate([frequency, frequency])[None]
    bf16, f32 = jnp.bfloat16, jnp.float32
    vmem, hbm = pl.BlockSpec(memory_space=pltpu.VMEM), pl.BlockSpec(memory_space=pl.ANY)
    chunked = (CHUNKS, token_count, piece)
    dma = pltpu.SemaphoreType.DMA
    layer_out, attended = pl.pallas_call(
        fused_kernel,
        out_shape=(
            jax.ShapeDtypeStruct((token_count, width), bf16),
            jax.ShapeDtypeStruct((token_count, w_query.shape[-1]), bf16),
        ),
        in_specs=[vmem] * 3 + [hbm] * 5 + [vmem] * 4,
        out_specs=(vmem, vmem),
        scratch_shapes=[
            pltpu.VMEM((4, token_count, width), bf16),
            pltpu.VMEM((half, width), bf16),
            pltpu.VMEM((hidden // 128, width, 256), bf16),
            pltpu.VMEM((hidden, width), bf16),
            pltpu.VMEM((hidden // 128, token_count, 128), bf16),
            pltpu.VMEM(chunked, bf16),
            pltpu.VMEM(chunked, bf16),
            pltpu.VMEM(chunked, bf16),
            pltpu.VMEM(chunked, f32),
            pltpu.VMEM(chunked, bf16),
            pltpu.VMEM(chunked, bf16),
            pltpu.VMEM(chunked, bf16),
            pltpu.VMEM((CHUNKS, half, piece), bf16),
            pltpu.VMEM((CHUNKS, half, piece), bf16),
            pltpu.VMEM(chunked, bf16),
            pltpu.VMEM(chunked, bf16),
            pltpu.VMEM((2, w_query.shape[1], out_width), bf16),
            pltpu.VMEM((6, token_count, out_width), bf16),
            pltpu.VMEM((token_count, 128), f32),
            pltpu.VMEM((token_count, 128), f32),
            pltpu.VMEM((reach + 1, token_count, 2 * head_dim), bf16),
            pltpu.VMEM((7, 1, token_count), jnp.int32),
            pltpu.VMEM((token_count, token_count), bf16),
            dma((16,)),
            dma((67,)), dma((67,)),
            dma((4,)), dma((4,)),
            dma((3,)), dma((3,)),
            dma((reach,)), dma((reach,)),
            dma((7,)), dma((7,)),
        ],
        compiler_params=pltpu.CompilerParams(
            collective_id=0, has_side_effects=True, vmem_limit_bytes=56 * 1024 * 1024
        ),
    )(
        tokens[0], routes[0].T, router_weights[0].T, w_gate[0, 0], w_up[0, 0], w_down[0, 0],
        w_query[0], w_keyval[0], gain_query, gain_key, segment_ids,
        frequency,
    )
    return (layer_out[None], attended[None])


def solution(mesh):
    in_specs = (
        P("section", "ep", None),
        P("section", "ep", None),
        P("section", "ep", None),
        P("section", "ep", None, None),
        P("section", "ep", None, None),
        P("section", "ep", None, None),
        P("section", "ep", None),
        P("section", "ep", None),
        P("section", None),
        P("section", None),
        P("section", "ep"),
    )
    out_specs = (P("section", "ep", None), P("section", "ep", None))
    return jax.shard_map(
        fused_on_device if mesh.shape["ep"] == 8 else on_device, mesh=mesh, in_specs=in_specs, out_specs=out_specs, check_vma=False
    )
```

```python
import math

import jax
import jax.numpy as jnp
from jax import lax
from jax.experimental import pallas as pl
from jax.experimental.pallas import tpu as pltpu
from jax.sharding import PartitionSpec as P

OWNERS = 4
SEG_MOST = 512


EPSILON = 1e-06
ROPE_BASE = 1000000.0
FAR_INDEX = 1073741824


def passed_along(block, axis, distance):
    devices = range(lax.axis_size(axis))
    route = [((i - distance) % len(devices), i) for i in devices]
    return lax.ppermute(block, axis, route)


def prefix(shard, axis, combine, identity):
    length, mine = (lax.axis_size(axis), lax.axis_index(axis))
    everything = jax.tree.map(lambda part: lax.all_gather(part, axis), shard)
    start = jax.tree.map(
        lambda part, zero: jnp.broadcast_to(jnp.asarray(zero, part.dtype), part.shape),
        shard,
        identity,
    )

    def step(k, before):
        reached = k < mine
        new = combine(before, jax.tree.map(lambda part: part[k], everything))
        return jax.tree.map(lambda a, b: jnp.where(reached, a, b), new, before)

    return lax.fori_loop(0, length, step, start)


def passed_along_2(value, axis, steps):
    count = lax.axis_size(axis)
    leading, last = (max(0, -steps), min(count, count - steps))
    return lax.ppermute(value, axis, [(source, source + steps) for source in range(leading, last)])


def rms_rows(values):
    return values * lax.rsqrt(jnp.mean(values * values, axis=-1, keepdims=True) + EPSILON)


def rotary(values, position):
    half_count = values.shape[-1] // 2
    frequency = ROPE_BASE ** (-(jnp.arange(half_count, dtype=jnp.float32) * 2.0) / values.shape[-1])
    angles = position.astype(jnp.float32)[:, None] * frequency[None, :]
    cosine = jnp.concatenate([jnp.cos(angles), jnp.cos(angles)], axis=-1)[:, None, :]
    sine = jnp.concatenate([jnp.sin(angles), jnp.sin(angles)], axis=-1)[:, None, :]
    turned = jnp.concatenate([-values[..., half_count:], values[..., :half_count]], axis=-1)
    return values * cosine + turned * sine


def feed_forward(row_block, gate_part, up_part, down_part):
    gate_proj = jnp.dot(row_block, gate_part, preferred_element_type=jnp.float32)
    up_proj = jnp.dot(row_block, up_part, preferred_element_type=jnp.float32)
    activated = (jax.nn.silu(gate_proj) * up_proj).astype(jnp.bfloat16)
    return jnp.dot(activated, down_part, preferred_element_type=jnp.float32)


def keep_later(earlier, later):
    same_id = earlier[0] == later[0]
    newer_id = later[0] > earlier[0]
    start_at = jnp.where(
        same_id, jnp.minimum(earlier[1], later[1]), jnp.where(newer_id, later[1], earlier[1])
    )
    return (jnp.maximum(earlier[0], later[0]), start_at)


def on_device(
    tokens,
    routes,
    router_weights,
    w_gate,
    w_up,
    w_down,
    w_query,
    w_keyval,
    gain_query,
    gain_key,
    segment_ids,
):
    device_count = lax.axis_size("ep")
    expert_count = device_count // OWNERS
    token_count = tokens.shape[1]
    model_width = tokens.shape[2]
    capacity = OWNERS * max(1, token_count // device_count)
    wide_tokens = tokens[0].astype(jnp.float32)
    normed = rms_rows(wide_tokens).astype(jnp.bfloat16)
    inside = routes[0] < expert_count
    has_route = jnp.any(inside, axis=-1)
    chosen = jnp.sum(jnp.where(inside, routes[0], 0), axis=-1)
    weight_kept = jnp.sum(jnp.where(inside, router_weights[0], 0.0), axis=-1)
    expert_ids = jnp.arange(expert_count, dtype=jnp.int32)
    member = ((chosen[:, None] == expert_ids[None, :]) & has_route[:, None]).astype(jnp.int32)
    token_ids = jnp.arange(token_count, dtype=jnp.int32)
    earlier = (token_ids[None, :] < token_ids[:, None]).astype(jnp.float32)
    ranks = jnp.dot(earlier, member.astype(jnp.float32)).astype(jnp.int32)
    rank_within = jnp.sum(ranks * member, axis=-1)
    slot_index = jnp.where(has_route, chosen * capacity + rank_within, -1)
    slot_ids = jnp.arange(expert_count * capacity, dtype=jnp.int32)
    placing = (slot_ids[:, None] == slot_index[None, :]).astype(jnp.bfloat16)
    packed = jnp.dot(placing, normed, preferred_element_type=jnp.float32).astype(jnp.bfloat16)
    gate_part = w_gate[0, 0]
    up_part = w_up[0, 0]
    down_part = w_down[0, 0]
    spread = jnp.broadcast_to(
        packed.reshape(expert_count, 1, capacity, model_width),
        (expert_count, OWNERS, capacity, model_width),
    ).reshape(device_count, capacity, model_width)
    received = lax.all_to_all(spread, "ep", split_axis=0, concat_axis=0, tiled=True)
    partial_out = feed_forward(
        received.reshape(-1, model_width), gate_part, up_part, down_part
    ).reshape(received.shape)
    returned_rows = lax.all_to_all(
        partial_out.astype(jnp.bfloat16), "ep", split_axis=0, concat_axis=0, tiled=True
    ).astype(partial_out.dtype)
    merged = jnp.sum(
        returned_rows.reshape(expert_count, OWNERS, capacity, model_width), axis=1
    ).reshape(expert_count * capacity, model_width)
    fetched_rows = jnp.take(merged, jnp.maximum(slot_index, 0), axis=0)
    expert_out = jnp.where(has_route[:, None], fetched_rows, 0.0)
    layer_out = (wide_tokens + weight_kept[:, None] * expert_out).astype(jnp.bfloat16)
    arrived = passed_along(layer_out, "section", 1)
    lifted = rms_rows(arrived.astype(jnp.float32)).astype(jnp.bfloat16)
    head_dim = gain_query.shape[-1]
    query_width = w_query.shape[-1]
    head_count = query_width // head_dim
    query_raw = jnp.dot(
        lifted,
        lax.all_gather(w_query[0], "ep", axis=0, tiled=True),
        preferred_element_type=jnp.float32,
    )
    keyval_raw = jnp.dot(
        lifted,
        lax.all_gather(w_keyval[0], "ep", axis=0, tiled=True),
        preferred_element_type=jnp.float32,
    )
    segment_row = segment_ids[0]
    first_index = lax.axis_index("ep") * token_count
    global_index = first_index + jnp.arange(token_count, dtype=jnp.int32)
    local_start = jnp.min(
        jnp.where(
            segment_row[None, :] == segment_row[:, None], global_index[None, :], FAR_INDEX
        ),
        axis=1,
    )
    empty_prior = (jnp.full((1,), -1, jnp.int32), jnp.full((1,), FAR_INDEX, jnp.int32))
    prior_id, prior_start = prefix(
        (segment_row[-1:], local_start[-1:]), "ep", keep_later, empty_prior
    )
    start_index = jnp.where(segment_row == prior_id[0], prior_start[0], local_start).astype(
        jnp.int32
    )
    position = global_index - start_index
    query = rotary(
        rms_rows(query_raw.reshape(token_count, head_count, head_dim)) * gain_query[0], position
    ).astype(jnp.bfloat16)
    key_part = rotary(rms_rows(keyval_raw[:, None, :head_dim]) * gain_key[0], position)[
        :, 0
    ].astype(jnp.bfloat16)
    value_part = keyval_raw[:, head_dim:].astype(jnp.bfloat16)
    key_value = jnp.concatenate([key_part, value_part], axis=-1)
    reach = (SEG_MOST - 1) // token_count + 1
    earlier_pieces = []
    for distance in range(1, reach + 1):
        earlier_pieces.append(passed_along_2(key_value, "ep", distance))
    window = jnp.concatenate(earlier_pieces[::-1] + [key_value], axis=0)
    key_index = (
        first_index - reach * token_count + jnp.arange((reach + 1) * token_count, dtype=jnp.int32)
    )
    query_rows = query.reshape(token_count * head_count, head_dim)
    query_index = jnp.repeat(global_index, head_count)
    query_start = jnp.repeat(start_index, head_count)
    score_scale = 1.0 / math.sqrt(head_dim)
    scores = (
        jnp.einsum(
            "qd,kd->qk", query_rows, window[:, :head_dim], preferred_element_type=jnp.float32
        )
        * score_scale
    )
    allowed = (key_index[None, :] <= query_index[:, None]) & (
        key_index[None, :] >= query_start[:, None]
    )
    probabilities = jnp.where(allowed, jnp.exp(scores), 0.0)
    total_mass = jnp.sum(probabilities, axis=-1)
    mixed = jnp.dot(
        probabilities.astype(jnp.bfloat16), window[:, head_dim:], preferred_element_type=jnp.float32
    )
    attended = (mixed / total_mass[:, None]).astype(jnp.bfloat16).reshape(token_count, query_width)
    return (layer_out[None], attended[None])


MESH = pl.DeviceIdType.MESH
CHUNKS = 4


def fused_kernel(
    tok_ref, route_ref, rw_ref, wg_hbm, wu_hbm, wd_hbm, wq_hbm, wkv_hbm,
    gq_ref, gk_ref, segrow_ref, freq_ref,
    lo_ref, att_ref,
    xbuf, other, wgu, wd, act, pd, py, pz, own, r1, r2y, r2z, sm, rm,
    lo, lbuf, wbuf, rbuf, scale_out, scale_in, kv, segs, place_s,
    load_sem, send_sem, recv_sem, l_send, l_recv, p_send, p_recv,
    kv_send, kv_recv, seg_send, seg_recv,
):
    f32, bf16 = jnp.float32, jnp.bfloat16
    section = lax.axis_index("section")
    sections = lax.axis_size("section")
    me = lax.axis_index("ep")
    count = lax.axis_size("ep")
    z, y = me // 2, me % 2
    expert = z // 2
    token_count, width = tok_ref.shape
    half = token_count // 2
    piece = width // CHUNKS
    y_peer = z * 2 + (1 - y)
    z_peer = (z // 2 * 2 + 1 - z % 2) * 2 + y
    mirror = lax.rem(z + 2, 4) * 2 + y
    following = lax.rem(section + 1, sections)
    preceding = lax.rem(section + sections - 1, sections)

    barrier = pltpu.get_barrier_semaphore()
    for k in range(1, 8):
        pl.semaphore_signal(
            barrier, inc=1, device_id=(section, lax.rem(me + k, count)), device_id_type=MESH
        )
    for k in range(4):
        pl.semaphore_signal(barrier, inc=1, device_id=(preceding, k * 2 + y), device_id_type=MESH)

    hidden_parts = wgu.shape[0]
    loads = []
    for j in range(hidden_parts):
        cols = pl.ds(j * 128, 128)
        loads.append((wg_hbm.at[:, cols], wgu.at[j, :, pl.ds(0, 128)]))
        loads.append((wu_hbm.at[:, cols], wgu.at[j, :, pl.ds(128, 128)]))
    loads.append((wd_hbm, wd))
    query_width = wq_hbm.shape[1]
    loads.append((wq_hbm, wbuf.at[y, :, pl.ds(0, query_width)]))
    loads.append((wkv_hbm, wbuf.at[y, :, pl.ds(query_width, wkv_hbm.shape[1])]))
    loads = [
        pltpu.make_async_copy(src, dst, load_sem.at[i]) for i, (src, dst) in enumerate(loads)
    ]
    for load in loads:
        load.start()

    def remote(src, dst, i, target):
        return pltpu.make_async_remote_copy(
            src_ref=src, dst_ref=dst, send_sem=send_sem.at[i], recv_sem=recv_sem.at[i],
            device_id=(section, target), device_id_type=MESH,
        )

    low, high = pl.ds(0, half), pl.ds(half, half)
    blocks = [pl.ds(b * (half // 4), half // 4) for b in range(4)]
    upper = [pl.ds(half + b * (half // 4), half // 4) for b in range(4)]
    c0 = [
        remote(other.at[s], xbuf.at[0, u], 27 + b, mirror)
        for b, (s, u) in enumerate(zip(blocks, upper))
    ]
    c1 = remote(xbuf.at[0, low], xbuf.at[1, low], 1, y_peer)
    c2 = remote(xbuf.at[0, low], xbuf.at[2, low], 2, z_peer)
    c3 = [remote(xbuf.at[0, u], xbuf.at[1, u], 31 + b, y_peer) for b, u in enumerate(upper)]
    c4 = [remote(xbuf.at[0, u], xbuf.at[2, u], 35 + b, z_peer) for b, u in enumerate(upper)]
    first, second = pl.ds(0, half // 2), pl.ds(half // 2, half // 2)
    c5 = remote(xbuf.at[1, first], xbuf.at[3, first], 5, z_peer)
    c7 = remote(xbuf.at[2, second], xbuf.at[3, second], 6, y_peer)
    c6 = [remote(xbuf.at[2, u], xbuf.at[3, u], 39 + b, y_peer) for b, u in enumerate(upper)]
    def parts(src, dst, base, target):
        return {
            (c, h): remote(
                src.at[c, pl.ds(h * half, half)], dst.at[c, pl.ds(h * half, half)],
                base + 2 * c + h, target(c),
            )
            for c in range(CHUNKS) for h in range(2)
        }

    first_hop = parts(pd, r1, 43, lambda c: z_peer if c < 2 else y_peer)
    to_y = parts(py, r2y, 51, lambda c: y_peer)
    to_z = parts(pz, r2z, 59, lambda c: z_peer)
    to_mirror = [remote(sm.at[c], rm.at[c], 19 + c, mirror) for c in range(CHUNKS)]
    weights = remote(wbuf.at[y], wbuf.at[y], 23, y_peer)
    weights_in = remote(wbuf.at[1 - y], wbuf.at[1 - y], 23, y_peer)

    squares = jnp.zeros((token_count, 1), f32)
    for c in range(CHUNKS):
        part = tok_ref[:, c * piece : (c + 1) * piece].astype(f32)
        squares += jnp.sum(part * part, axis=-1, keepdims=True)
    inverse = lax.rsqrt(squares / width + EPSILON)
    lane_i = lax.broadcasted_iota(jnp.int32, (token_count, token_count), 1)
    row_i = lax.broadcasted_iota(jnp.int32, (token_count, token_count), 0)

    def column(row):
        return jnp.sum(jnp.where(lane_i == row_i, row, 0.0), axis=-1, keepdims=True)

    routes = route_ref[...]
    inside = routes < 2
    has_route = column(jnp.sum(jnp.where(inside, 1.0, 0.0), axis=0, keepdims=True))
    chosen = column(
        jnp.sum(jnp.where(inside, routes.astype(f32), 0.0), axis=0, keepdims=True)
    )
    weight = column(jnp.sum(jnp.where(inside, rw_ref[...], 0.0), axis=0, keepdims=True))
    group = jnp.where(chosen == expert.astype(f32), 0.0, 1.0)
    lane = lane_i.astype(f32)
    groups = jnp.where(lane == group, has_route, 0.0)
    before = jnp.where(lane_i < row_i, 1.0, 0.0)
    ranks = jnp.dot(before.astype(bf16), groups.astype(bf16), preferred_element_type=f32)
    rank = jnp.sum(ranks * groups, axis=-1, keepdims=True)
    placing = jnp.where(lane == group * half + rank, has_route, 0.0).astype(bf16)
    place_s[...] = placing
    for c in range(CHUNKS):
        cols = slice(c * piece, (c + 1) * piece)
        normed = (tok_ref[:, cols].astype(f32) * inverse).astype(bf16)
        packed = lax.dot_general(
            placing, normed, (((0,), (0,)), ((), ())), preferred_element_type=f32
        ).astype(bf16)
        xbuf[0, 0:half, cols] = packed[:half]
        other[:, cols] = packed[half:]

    pl.semaphore_wait(barrier, 11)
    for copy in c0:
        copy.start()
    c1.start()
    c2.start()
    seg_copies = []
    for k in range(1, 8):
        copy = pltpu.make_async_remote_copy(
            src_ref=segrow_ref, dst_ref=segs.at[k - 1],
            send_sem=seg_send.at[k - 1], recv_sem=seg_recv.at[k - 1],
            device_id=(section, lax.rem(me + k, count)), device_id_type=MESH,
        )
        copy.start()
        seg_copies.append(copy)

    def expert_rows(q):
        def step(j, carry):
            both = jnp.dot(xbuf[q], wgu[j], preferred_element_type=f32)
            gate, up = both[:, :128], both[:, 128:]
            act[j] = (gate / (1.0 + jnp.exp(-gate)) * up).astype(bf16)
            return carry

        lax.fori_loop(0, hidden_parts, step, 0)
        return jnp.concatenate([act[j] for j in range(hidden_parts)], axis=-1)

    def down(rows, c):
        return jnp.dot(
            rows, wd[:, c * piece : (c + 1) * piece], preferred_element_type=f32
        )

    for b in range(4):
        c0[b].wait_recv()
        c3[b].start()
        c4[b].start()
        if b == 1:
            c1.wait_recv()
            c5.start()
            c2.wait_recv()
            c7.start()
    for b in range(4):
        c4[b].wait_recv()
        c6[b].start()
    for load in loads:
        load.wait()
    rows = expert_rows(0)
    for c in range(CHUNKS):
        own[c] = down(rows, c)
    rows = expert_rows(2)
    for c in range(CHUNKS):
        pz[c] = down(rows, c).astype(bf16)
        if c < 2:
            to_z[c, 1].start()
    for copy in c3:
        copy.wait_recv()
    rows = expert_rows(1)
    for c in (2, 3, 0, 1):
        py[c] = down(rows, c).astype(bf16)
        if c >= 2:
            to_y[c, 1].start()
    c5.wait_recv()
    c7.wait_recv()
    for copy in c6:
        copy.wait_recv()
    rows = expert_rows(3)
    order = (0, 2, 1, 3)
    for c in order:
        pd[c] = down(rows, c).astype(bf16)
        first_hop[c, 1].start()
    for c in order:
        first_hop[c, 0].start()
    for c in order:
        (to_z if c < 2 else to_y)[c, 0].start()
    for h in (1, 0):
        part = slice(h * half, (h + 1) * half)
        for c in order:
            first_hop[c, h].wait_recv()
            out, copies = (py, to_y) if c < 2 else (pz, to_z)
            out[c, part] = (out[c, part].astype(f32) + r1[c, part].astype(f32)).astype(bf16)
            copies[c, h].start()
    weights.start()
    for h in (1, 0):
        part = slice(h * half, (h + 1) * half)
        for c in order:
            to_y[c, h].wait_recv()
            to_z[c, h].wait_recv()
            total = own[c, part] + r2y[c, part].astype(f32) + r2z[c, part].astype(f32)
            if h:
                sm[c] = total.astype(bf16)
                to_mirror[c].start()
            else:
                own[c, part] = total

    def onward(c):
        return pltpu.make_async_remote_copy(
            src_ref=lo.at[c], dst_ref=lbuf.at[z], send_sem=l_send.at[c], recv_sem=l_recv.at[z],
            device_id=(following, c * 2 + y), device_id_type=MESH,
        )

    squares = jnp.zeros((token_count, 1), f32)
    for c in order:
        to_mirror[c].wait_recv()
        merged = jnp.concatenate([own[c][:half].astype(bf16), rm[c]], axis=0)
        spread = jnp.dot(place_s[...], merged, preferred_element_type=f32)
        cols = slice(c * piece, (c + 1) * piece)
        result = (tok_ref[:, cols].astype(f32) + weight * spread).astype(bf16)
        lo[c] = result
        onward(c).start()
        lo_ref[:, cols] = result
        wide = result.astype(f32)
        squares += jnp.sum(wide * wide, axis=-1, keepdims=True)
    scale_out[...] = jnp.broadcast_to(
        lax.rsqrt(squares / width + EPSILON), scale_out.shape
    )
    scale_copy = pltpu.make_async_remote_copy(
        src_ref=scale_out, dst_ref=scale_in, send_sem=send_sem.at[24], recv_sem=recv_sem.at[24],
        device_id=(following, me), device_id_type=MESH,
    )
    scale_copy.start()

    for copy in seg_copies:
        copy.wait_recv()
    own_row = segrow_ref[...].astype(f32)
    mine = column(own_row)
    start = jnp.sum(jnp.where(own_row < mine, 1.0, 0.0), axis=-1, keepdims=True)
    for k in range(7):
        start += jnp.sum(jnp.where(segs[k].astype(f32) < mine, 1.0, 0.0), axis=-1, keepdims=True)
    index = (
        lax.broadcasted_iota(jnp.int32, (token_count, 1), 0) + me * token_count
    ).astype(f32)
    angles = (index - start) * freq_ref[...]
    head_dim = gq_ref.shape[-1]
    cosine = jnp.cos(angles)
    lanes = lax.broadcasted_iota(jnp.int32, (token_count, head_dim), 1)
    sine = jnp.where(lanes < head_dim // 2, -1.0, 1.0) * jnp.sin(angles)

    weights_in.wait_recv()

    def project(rows):
        result = jnp.dot(rows[:, : piece // 2], wbuf[0], preferred_element_type=f32)
        result += jnp.dot(rows[:, piece // 2 :], wbuf[1], preferred_element_type=f32)
        return result

    def arrival(source):
        return pltpu.make_async_remote_copy(
            src_ref=lo.at[0], dst_ref=lbuf.at[source], send_sem=l_send.at[0],
            recv_sem=l_recv.at[source], device_id=(preceding, source * 2 + y),
            device_id_type=MESH,
        )

    z_side = z // 2 * 2 + 1 - z % 2

    def partial_copy(slot, h, target):
        rows = pl.ds(h * half, half)
        return pltpu.make_async_remote_copy(
            src_ref=rbuf.at[3 + slot, rows], dst_ref=rbuf.at[slot, rows],
            send_sem=p_send.at[2 * slot + h], recv_sem=p_recv.at[2 * slot + h],
            device_id=(section, target), device_id_type=MESH,
        )

    targets = (z_peer, z_peer, mirror)
    partial_copies = [[partial_copy(i, h, targets[i]) for h in range(2)] for i in range(3)]
    source = lax.rem(z_side + 2, 4)
    arrival(source).wait_recv()
    rbuf[4] = project(lbuf[source]).astype(bf16)
    for copy in partial_copies[1]:
        copy.start()
    source = lax.rem(z + 2, 4)
    arrival(source).wait_recv()
    crossing = project(lbuf[source])
    arrival(z_side).wait_recv()
    rbuf[3] = project(lbuf[z_side]).astype(bf16)
    for copy in partial_copies[0]:
        copy.start()
    for h in range(2):
        part = slice(h * half, (h + 1) * half)
        partial_copies[1][h].wait_recv()
        rbuf[5, part] = (crossing[part] + rbuf[1, part].astype(f32)).astype(bf16)
        partial_copies[2][h].start()
    arrival(z).wait_recv()
    mixed = project(lbuf[z])
    scale_copy.wait_recv()
    for copy in partial_copies[0]:
        copy.wait_recv()
    mixed += rbuf[0].astype(f32)
    for copy in partial_copies[2]:
        copy.wait_recv()
    mixed += rbuf[2].astype(f32)
    mixed *= scale_in[:, 0:1]

    def turn(values, gain):
        values = values * lax.rsqrt(jnp.mean(values * values, axis=-1, keepdims=True) + EPSILON)
        values = values * gain
        return values * cosine + pltpu.roll(values, head_dim // 2, 1) * sine

    key = turn(mixed[:, query_width : query_width + head_dim], gk_ref[...]).astype(bf16)
    kv[0, :, 0:head_dim] = key
    kv[0, :, head_dim:] = mixed[:, query_width + head_dim :].astype(bf16)
    reach = kv.shape[0] - 1
    kv_copies = []
    for k in range(1, reach + 1):
        copy = pltpu.make_async_remote_copy(
            src_ref=kv.at[0], dst_ref=kv.at[k], send_sem=kv_send.at[k - 1],
            recv_sem=kv_recv.at[k - 1], device_id=(section, lax.rem(me + k, count)),
            device_id_type=MESH,
        )
        copy.start()
        kv_copies.append(copy)
    queries = [
        turn(mixed[:, h * head_dim : (h + 1) * head_dim], gq_ref[...]).astype(bf16)
        for h in range(query_width // head_dim)
    ]
    for copy in kv_copies:
        copy.wait_recv()
    key_count = (reach + 1) * token_count
    place = lax.broadcasted_iota(jnp.int32, (1, key_count), 1)
    slot = place // token_count
    key_index = (lax.rem(me - slot + count, count) * token_count + place % token_count).astype(f32)
    allowed = (key_index <= index) & (key_index >= start)
    everything = kv[...].reshape(key_count, 2 * head_dim)
    keys, values = everything[:, :head_dim], everything[:, head_dim:]
    for h, query in enumerate(queries):
        scores = lax.dot_general(
            query, keys, (((1,), (1,)), ((), ())), preferred_element_type=f32
        ) * (1.0 / math.sqrt(head_dim))
        probs = jnp.where(allowed, jnp.exp(scores), 0.0)
        mass = jnp.sum(probs, axis=-1, keepdims=True)
        out = jnp.dot(probs.astype(bf16), values, preferred_element_type=f32) / mass
        att_ref[:, h * head_dim : (h + 1) * head_dim] = out.astype(bf16)

    for copy in [c1, c2, c5, c7, weights, scale_copy, *c0, *c3, *c4, *c6]:
        copy.wait_send()
    for copies in (first_hop, to_y, to_z):
        for copy in copies.values():
            copy.wait_send()
    for copy in to_mirror + seg_copies + kv_copies + sum(partial_copies, []):
        copy.wait_send()
    for c in range(CHUNKS):
        onward(c).wait_send()


def fused_on_device(
    tokens, routes, router_weights, w_gate, w_up, w_down, w_query, w_keyval,
    gain_query, gain_key, segment_ids,
):
    token_count, width = tokens.shape[1:]
    half = token_count // 2
    piece = width // CHUNKS
    hidden = w_gate.shape[-1]
    head_dim = gain_query.shape[-1]
    out_width = w_query.shape[-1] + w_keyval.shape[-1]
    reach = (SEG_MOST - 1) // token_count + 1
    half_count = head_dim // 2
    frequency = ROPE_BASE ** (-(jnp.arange(half_count, dtype=jnp.float32) * 2.0) / head_dim)
    frequency = jnp.concatenate([frequency, frequency])[None]
    bf16, f32 = jnp.bfloat16, jnp.float32
    vmem, hbm = pl.BlockSpec(memory_space=pltpu.VMEM), pl.BlockSpec(memory_space=pl.ANY)
    chunked = (CHUNKS, token_count, piece)
    dma = pltpu.SemaphoreType.DMA
    layer_out, attended = pl.pallas_call(
        fused_kernel,
        out_shape=(
            jax.ShapeDtypeStruct((token_count, width), bf16),
            jax.ShapeDtypeStruct((token_count, w_query.shape[-1]), bf16),
        ),
        in_specs=[vmem] * 3 + [hbm] * 5 + [vmem] * 4,
        out_specs=(vmem, vmem),
        scratch_shapes=[
            pltpu.VMEM((4, token_count, width), bf16),
            pltpu.VMEM((half, width), bf16),
            pltpu.VMEM((hidden // 128, width, 256), bf16),
            pltpu.VMEM((hidden, width), bf16),
            pltpu.VMEM((hidden // 128, token_count, 128), bf16),
            pltpu.VMEM(chunked, bf16),
            pltpu.VMEM(chunked, bf16),
            pltpu.VMEM(chunked, bf16),
            pltpu.VMEM(chunked, f32),
            pltpu.VMEM(chunked, bf16),
            pltpu.VMEM(chunked, bf16),
            pltpu.VMEM(chunked, bf16),
            pltpu.VMEM((CHUNKS, half, piece), bf16),
            pltpu.VMEM((CHUNKS, half, piece), bf16),
            pltpu.VMEM(chunked, bf16),
            pltpu.VMEM(chunked, bf16),
            pltpu.VMEM((2, w_query.shape[1], out_width), bf16),
            pltpu.VMEM((6, token_count, out_width), bf16),
            pltpu.VMEM((token_count, 128), f32),
            pltpu.VMEM((token_count, 128), f32),
            pltpu.VMEM((reach + 1, token_count, 2 * head_dim), bf16),
            pltpu.VMEM((7, 1, token_count), jnp.int32),
            pltpu.VMEM((token_count, token_count), bf16),
            dma((16,)),
            dma((67,)), dma((67,)),
            dma((4,)), dma((4,)),
            dma((6,)), dma((6,)),
            dma((reach,)), dma((reach,)),
            dma((7,)), dma((7,)),
        ],
        compiler_params=pltpu.CompilerParams(
            collective_id=0, has_side_effects=True, vmem_limit_bytes=56 * 1024 * 1024
        ),
    )(
        tokens[0], routes[0].T, router_weights[0].T, w_gate[0, 0], w_up[0, 0], w_down[0, 0],
        w_query[0], w_keyval[0], gain_query, gain_key, segment_ids,
        frequency,
    )
    return (layer_out[None], attended[None])


def solution(mesh):
    in_specs = (
        P("section", "ep", None),
        P("section", "ep", None),
        P("section", "ep", None),
        P("section", "ep", None, None),
        P("section", "ep", None, None),
        P("section", "ep", None, None),
        P("section", "ep", None),
        P("section", "ep", None),
        P("section", None),
        P("section", None),
        P("section", "ep"),
    )
    out_specs = (P("section", "ep", None), P("section", "ep", None))
    return jax.shard_map(
        fused_on_device if mesh.shape["ep"] == 8 else on_device, mesh=mesh, in_specs=in_specs, out_specs=out_specs, check_vma=False
    )
```
